256 devices in a mesh: dp: 32 (over z_lo, y, core), st: 8 (over x, z_hi).
Axes of the slice: x: 4, y: 4, z: 8 (z_hi: 2, z_lo: 4; z = z_hi * 4 + z_lo), core: 2. Of those that a mesh axis runs over, the one named last changes fastest.
Arguments:
- hidden: bfloat16 [32768, 3584], P(('dp', 'st')), may hold values from -12 to 12, as said below
- w_down: bfloat16 [3584, 1536], P(None, 'st'), as said below
- norm_gain: float32 [1536], P('st'), may hold values from 0.5 to 1.5
- w_up: bfloat16 [1536, 12288], P(None, 'st'), may hold values from -0.15625 to 0.15625
- grad_query: bfloat16 [32768, 12288], P('dp', 'st'), may hold values from -0.078125 to 0.078125
Outputs:
- grad_down: float32 [3584, 1536], P('dp', 'st')
- grad_up: float32 [1536, 12288], P('dp', 'st')
- grad_gain: float32 [1536], P('st')
The draws below stay inside these ranges and needn't reach their ends.
Inputs may be any that keep to these rules, and one draw needn't show every extreme that they name: hidden states of order one. `w_down`: entries of order D ** -0.5.
All inputs are finite; a program needn't handle non-finite values.
Results may differ from the reference program's by a relative error of at most 0.0029.
Values may be sent and summed in bfloat16 or wider, within the bound.
A program may use at most 128 MiB of HBM per device.

```python
import jax
import jax.numpy as jnp
from jax import lax

D = 3584
L = 1536
H = 64
HEAD = 192
TOKENS = 32768


def draw_hidden(key, part):
    key = jax.random.fold_in(key, 11)
    scale_key, value_key = jax.random.split(key)
    row_scale = jnp.exp(jax.random.uniform(scale_key, (TOKENS, 1), jnp.float32, jnp.log(0.3), jnp.log(3.0)))
    values = jax.random.normal(value_key, (TOKENS, D), jnp.float32)
    return jnp.clip(values * row_scale, -12.0, 12.0).astype(jnp.bfloat16)


def draw_w_down(key, part):
    key = jax.random.fold_in(key, 23)
    jitter_key, value_key = jax.random.split(key)
    trend = 0.5 * 3.0 ** (jnp.arange(L, dtype=jnp.float32) / max(L - 1, 1))
    jitter = jnp.exp(jax.random.uniform(jitter_key, (L,), jnp.float32, jnp.log(0.5), jnp.log(2.0)))
    values = jnp.clip(jax.random.normal(value_key, (D, L), jnp.float32), -6.0, 6.0)
    return (values * D ** (-0.5) * trend * jitter).astype(jnp.bfloat16)


def steps_of(own_key, extent, cuts, smallest, top_value):
    def one(position, shards_of):
        heights = jax.random.uniform(jax.random.fold_in(jax.random.fold_in(own_key, 6), position), (shards_of,), jnp.float32, smallest / len(cuts), top_value / len(cuts))
        return jnp.repeat(jnp.exp(heights), extent[position] // shards_of).reshape((-1,) + (1,) * (len(extent) - position - 1))

    factor_of = one(*cuts[0])
    for cut in cuts[1:]:
        factor_of = factor_of * one(*cut)
    return factor_of


def gaussian(own_key, dims, spread, reach, cuts=(), kind=jnp.bfloat16):
    result = jax.random.normal(own_key, dims, jnp.float32) * spread
    if len(cuts) > 0:
        result = steps_of(own_key, dims, cuts, -0.22, 0.18) * result
    return jnp.clip(result, min=-reach, max=reach).astype(kind)


def setup_inputs(seed: int = 0) -> dict:
    key_list = jax.random.split(jax.random.key(seed), 6)
    return {
        "hidden": draw_hidden(jax.random.fold_in(key_list[5], 71), 0),
        "w_down": draw_w_down(jax.random.fold_in(key_list[5], 71), 0),
        "norm_gain": jnp.clip(1.0 + 0.1 * jax.random.normal(key_list[2], (L,), jnp.float32), 0.5, 1.5),
        "w_up": gaussian(key_list[3], (L, H * HEAD), L ** -0.5, 0.15625, ((1, 8),)),
        "grad_query": gaussian(key_list[4], (TOKENS, H * HEAD), 0.005, 0.078125, ((0, 32), (1, 8))),
    }


def reference(hidden, w_down, norm_gain, w_up, grad_query):
    latent = jnp.dot(hidden, w_down, preferred_element_type=jnp.float32)
    inverse = lax.rsqrt(lax.optimization_barrier(jnp.mean(latent * latent, axis=1, keepdims=True)) + 1e-06)
    normed = (latent * inverse * norm_gain).astype(jnp.bfloat16)
    grad_up = jnp.dot(normed.T, grad_query, preferred_element_type=jnp.float32)
    grad_normed = jnp.dot(grad_query, w_up.T, preferred_element_type=jnp.float32)
    inner = lax.optimization_barrier(jnp.sum(norm_gain * grad_normed * latent, axis=1, keepdims=True))
    grad_latent = (inverse * norm_gain * grad_normed - latent * inverse ** 3 * inner / L).astype(jnp.bfloat16)
    grad_down = jnp.dot(hidden.T, grad_latent, preferred_element_type=jnp.float32)
    grad_gain = lax.optimization_barrier(jnp.sum(grad_normed * latent * inverse, axis=0))
    return (grad_down, grad_up, grad_gain)
```

```python
import functools

import jax
import jax.numpy as jnp
from jax import lax
from jax.experimental import pallas as pl
from jax.experimental.pallas import tpu as pltpu
from jax.sharding import PartitionSpec as P

L = 1536
MESH = pl.DeviceIdType.MESH
F32 = jnp.float32
BF16 = jnp.bfloat16
SUB = 112


def coordinates():
    dp = lax.axis_index("dp")
    st = lax.axis_index("st")
    zl, y, c = dp // 8, lax.rem(dp // 2, 4), lax.rem(dp, 2)
    x, zh = st // 2, lax.rem(st, 2)
    return x, y, zh * 4 + zl, c


def device(x, y, z, c):
    x, y, z, c = lax.rem(x + 8, 4), lax.rem(y + 8, 4), lax.rem(z + 16, 8), lax.rem(c + 2, 2)
    return ((lax.rem(z, 4) * 4 + y) * 2 + c, x * 2 + z // 4)


def send(src, dst, send_sem, recv_sem, to):
    copy = pltpu.make_async_remote_copy(
        src_ref=src, dst_ref=dst, send_sem=send_sem, recv_sem=recv_sem, device_id=to, device_id_type=MESH
    )
    copy.start()
    return copy


def meet(peers):
    barrier = pltpu.get_barrier_semaphore()
    for peer in peers:
        pl.semaphore_signal(barrier, inc=1, device_id=peer, device_id_type=MESH)
    pl.semaphore_wait(barrier, len(peers))


def front(
    hid, wd, gain, wup, gq, nt_out, gl_out, gp_out, ht_out,
    hk, xb, gb, w, snd, rcv, own, zs, zr, lp, lx, nat,
    loc_sem, x_s, x_r, g_s, g_r, h_s, h_r, n_s, n_r, q_s, q_r,
    za_s, za_r, zb_s, zb_r, yp_s, yp_r, ym_s, ym_r, yf_s, yf_r, l_s, l_r,
):
    x, y, z, c = coordinates()
    zh, zl = z // 4, lax.rem(z, 4)
    st = x * 2 + zh
    st_peers = [(dx, dz) for dz in (0, 4) for dx in (0, 1, 2, 3) if (dx, dz) != (0, 0)]
    s = 1 - 2 * c
    core_peer = device(x, y, z, c + 1)
    up_z, down_z = device(x, y, z + s, c), device(x, y, z - s, c)
    up_y, down_y = device(x, y + 1, z, c), device(x, y - 1, z, c)
    meet(
        [device(x + dx, y, z + dz, c) for dx, dz in st_peers] + [core_peer, up_z, down_z, up_y, down_y]
    )
    sends = []
    row = pl.multiple_of(c * 1792 + (y * 4 + zl) * SUB, 16)
    piece = wd.at[pl.ds(row, SUB)]
    own_piece = pltpu.make_async_copy(piece, xb.at[x], loc_sem.at[0])
    own_piece.start()
    x_copies = [
        send(piece, xb.at[x], x_s.at[d - 1], x_r.at[d - 1], device(x + d, y, z, c)) for d in (2, 1, 3)
    ]
    other_k = hid.at[:, pl.ds(pl.multiple_of((1 - c) * 1792, 128), 1792)]
    own_k = hid.at[:, pl.ds(pl.multiple_of(c * 1792, 128), 1792)]
    h_copy = send(other_k, hk.at[c], h_s, h_r, core_peer)
    own_hid = pltpu.make_async_copy(own_k, hk.at[c], loc_sem.at[1])
    own_hid.start()
    own_gain = pltpu.make_async_copy(gain, gb.at[st], loc_sem.at[2])
    own_gain.start()
    g_copies = [
        send(gain, gb.at[st], g_s.at[i], g_r.at[i], device(x + dx, y, z + dz, c))
        for i, (dx, dz) in enumerate(st_peers)
    ]
    sends += x_copies + [h_copy] + g_copies

    def cotangent(owner, store):
        def tile(i, _):
            cols = pl.ds(pl.multiple_of(i * 256, 256), 256)
            store(
                cols,
                lax.dot_general(
                    gq[pl.ds(pl.multiple_of(owner * 256, 256), 256), :],
                    wup[cols, :],
                    (((1,), (1,)), ((), ())),
                    preferred_element_type=F32,
                ),
            )
            return 0

        lax.fori_loop(0, 6, tile, 0)

    far = pl.ds(pl.multiple_of((1 - zh) * 128, 128), 128)
    near = pl.ds(pl.multiple_of(zh * 128, 128), 128)
    n_copies = {}

    def partial_for(j, d):
        def store(cols, value):
            snd[j, :, cols] = value.astype(BF16)

        cotangent(lax.rem(x + d, 4), store)
        n_copies[j, 0] = send(
            snd.at[j, far], rcv.at[j, far], n_s.at[j, 0], n_r.at[j, 0], device(x + d, y, z, c)
        )

    partial_for(0, 2)

    own_piece.wait()
    for copy in x_copies:
        copy.wait_recv()

    def unit(zz, yy):
        zz, yy = lax.rem(zz + 16, 8), lax.rem(yy + 8, 4)
        rows = pl.multiple_of((yy * 4 + lax.rem(zz, 4)) * SUB, 16)
        return w.at[zz // 4, pl.ds(rows, SUB)]

    my_rows = pl.ds(pl.multiple_of((y * 4 + zl) * SUB, 16), SUB)
    for i in range(4):
        w[zh, my_rows, i * 192 : (i + 1) * 192] = xb[i]

    owners = [z, z - s, z + s, z - 2 * s, z + 2 * s, z - 3 * s, z + 3 * s, z - 4 * s]
    za, zb, yp, ym, yf = {}, {}, {}, {}, {}

    def pass_on(k):
        here = unit(owners[k], y)
        if k == 0 or (k % 2 == 1 and k < 7):
            i = (k + 1) // 2
            za[i] = send(here, here, za_s.at[i], za_r.at[i], up_z)
        if k == 0 or (k % 2 == 0 and k < 6):
            i = k // 2
            zb[i] = send(here, here, zb_s.at[i], zb_r.at[i], down_z)
        yp[k] = send(here, here, yp_s.at[k], yp_r.at[k], up_y)
        ym[k] = send(here, here, ym_s.at[k], ym_r.at[k], down_y)

    def forward(k):
        yp[k].wait_recv()
        ym[k].wait_recv()
        if k % 2 == 0:
            there = unit(owners[k], y - 1)
            yf[k] = send(there, there, yf_s.at[k], yf_r.at[k], up_y)
        else:
            there = unit(owners[k], y + 1)
            yf[k] = send(there, there, yf_s.at[k], yf_r.at[k], down_y)

    pass_on(0)
    partial_for(1, 1)
    partial_for(2, 3)
    for j, d in enumerate((2, 1, 3)):
        n_copies[j, 1] = send(
            snd.at[j, near], rcv.at[j, near], n_s.at[j, 1], n_r.at[j, 1], device(x + d, y, z, c)
        )

    def keep(cols, value):
        own[:, cols] = value

    za[0].wait_recv()
    pass_on(1)
    zb[0].wait_recv()
    pass_on(2)
    cotangent(x, keep)

    def turn(i, _):
        cols = pl.ds(pl.multiple_of(i * 128, 128), 128)
        ht_out[cols, :] = hid[:, cols].astype(F32).T.astype(BF16)
        return 0

    lax.fori_loop(0, 28, turn, 0)
    forward(0)
    q_copy = None
    for k in range(3, 8):
        if k % 2 == 1:
            za[k // 2].wait_recv()
        else:
            zb[k // 2 - 1].wait_recv()
        pass_on(k)
        forward(k - 2)
        if k == 5:
            for j in range(3):
                n_copies[j, 0].wait_recv()
            total = own[far, :]
            for j in range(3):
                total = total + rcv[j, far, :].astype(F32)
            zs[...] = total.astype(zs.dtype)
            q_copy = send(zs, zr, q_s, q_r, device(x, y, z + 4, c))
    forward(6)
    forward(7)
    for k in range(8):
        yf[k].wait_recv()
    h_copy.wait_recv()
    own_hid.wait()

    for half in range(2):

        def tile(i, _):
            cols = pl.ds(pl.multiple_of(i * 256, 256), 256)
            value = jnp.dot(
                hk[...].reshape(256, 1792), w[half, :, cols], preferred_element_type=F32
            )
            lp[:, half, :, cols] = value.reshape(2, 128, 256)
            return 0

        lax.fori_loop(0, 3, tile, 0)
    l_copy = send(lp.at[1 - c], lx, l_s, l_r, core_peer)

    own_gain.wait()
    for copy in g_copies:
        copy.wait_recv()
    for j in range(3):
        n_copies[j, 1].wait_recv()
    q_copy.wait_recv()
    l_copy.wait_recv()
    for half in range(2):
        for i in range(4):
            piece_cols = pl.ds(i * 192, 192)
            at = i * 384 + half * 192
            nat[:, at : at + 192] = lp[c, half, :, piece_cols] + lx[half, :, piece_cols]
    for i in range(8):
        gp_out[:, i * 192 : (i + 1) * 192] = jnp.broadcast_to(gb[i], (8, 192))
    gains = gp_out[0:1, :]
    latent = nat[...]
    inverse = lax.rsqrt(jnp.sum(latent * latent, axis=1, keepdims=True) / L + 1e-06)
    total = own[near, :] + zr[...].astype(F32)
    for j in range(3):
        total = total + rcv[j, near, :].astype(F32)
    own[0:128, :] = total
    inner = jnp.sum(gains * total * latent, axis=1, keepdims=True)
    factor = inverse**3 * inner / L
    for i in range(12):
        cols = pl.ds(i * 128, 128)
        lat, cot, g = nat[:, cols], own[0:128, cols], gp_out[0:1, cols]
        gl_out[:, cols] = (inverse * g * cot - lat * factor).astype(BF16)
        nt_out[cols, :] = (lat * inverse * g).T.astype(BF16)
        gp_out[:, cols] = jnp.broadcast_to(jnp.sum(cot * lat * inverse, axis=0, keepdims=True), (8, 128))
    for copy in (
        sends
        + [n_copies[j, h] for j in range(3) for h in range(2)]
        + [q_copy, l_copy]
        + list(za.values()) + list(zb.values()) + list(yp.values()) + list(ym.values()) + list(yf.values())
    ):
        copy.wait_send()


def back(
    nt, gl, gp, ht, gq, gd_out, gu_out, gg_out,
    ntx, gx, g, hr, gla, gpa, xs, xr, zs, zr, us, ur, vs, vr,
    loc_sem, c_s, c_r, hs, hrs, gl_s, gl_r, gf_s, gf_r, gp_s, gp_r,
    z4_s, z4_r, na_s, na_r, nb_s, nb_r, d_s, d_r, e_s, e_r, u_s, u_r, v_s, v_r,
):
    x, y, z, c = coordinates()
    zh, zl = z // 4, lax.rem(z, 4)
    st = x * 2 + zh
    core_peer = device(x, y, z, c + 1)
    yc = [(dy, dc) for dy in (0, 1, 2, 3) for dc in (0, 1) if (dy, dc) != (0, 0)]
    meet(
        [device(x + d, y, z, c) for d in (1, 2, 3)]
        + [device(x, y, z + d, c) for d in range(1, 8)]
        + [device(x, y + dy, z, c + dc) for dy, dc in yc]
    )
    sends = []
    mine = y * 2 + c
    lanes_c = pl.ds(pl.multiple_of(c * 128, 128), 128)
    nt_core = send(nt.at[:, 1 - c], ntx.at[st, :, :, lanes_c], c_s.at[0], c_r.at[0], core_peer)
    nt_own = pltpu.make_async_copy(nt.at[:, c], ntx.at[st, :, :, lanes_c], loc_sem.at[0])
    nt_own.start()
    gl_copies = [
        send(gl, gla.at[mine], gl_s.at[i], gl_r.at[i], device(x, y + dy, z, c)) for i, dy in enumerate((2, 1, 3))
    ]
    gp_copies = [
        send(gp, gpa.at[mine], gp_s.at[i], gp_r.at[i], device(x, y + dy, z, c + dc))
        for i, (dy, dc) in enumerate(yc)
    ]
    gl_core = send(gl, gla.at[mine], gf_s.at[3], gf_r.at[3], core_peer)
    gl_own = pltpu.make_async_copy(gl, gla.at[mine], loc_sem.at[1])
    gl_own.start()
    gp_own = pltpu.make_async_copy(gp, gpa.at[mine], loc_sem.at[2])
    gp_own.start()
    nt_own.wait()
    nt_core.wait_recv()
    z4 = send(ntx.at[st], ntx.at[st], z4_s, z4_r, device(x, y, z + 4, c))
    na = [
        send(ntx.at[st], ntx.at[st], na_s.at[i], na_r.at[i], device(x + d, y, z, c))
        for i, d in enumerate((2, 1, 3))
    ]
    lanes_me = pl.ds(pl.multiple_of(mine * 128, 128), 128)
    h_copies = []
    for i, (dy, dc) in enumerate(yc):
        ty, tc = lax.rem(y + dy, 4), lax.rem(c + dc, 2)
        h_copies.append(
            send(ht.at[:, ty, tc], hr.at[:, :, lanes_me], hs.at[i], hrs.at[i], device(x, y + dy, z, c + dc))
        )
    h_own = pltpu.make_async_copy(ht.at[:, y, c], hr.at[:, :, lanes_me], loc_sem.at[3])
    h_own.start()
    gq_core = send(gq, gx.at[:, c], c_s.at[1], c_r.at[1], core_peer)
    gq_own = pltpu.make_async_copy(gq, gx.at[:, c], loc_sem.at[4])
    gq_own.start()
    sends += [nt_core, gl_core, z4, gq_core] + gl_copies + gp_copies + na + h_copies

    gl_fwd = []
    for i, dy in enumerate((2, 1, 3)):
        gl_copies[i].wait_recv()
        from_y = gla.at[lax.rem(y - dy + 4, 4) * 2 + c]
        gl_fwd.append(send(from_y, from_y, gf_s.at[i], gf_r.at[i], core_peer))
    sends += gl_fwd
    z4.wait_recv()
    other = ntx.at[st + 1 - 2 * zh]
    nb = [
        send(other, other, nb_s.at[i], nb_r.at[i], device(x + d, y, z, c)) for i, d in enumerate((2, 1, 3))
    ]
    sends += nb

    def product(zz, cols):
        value = None
        for i in range(4):
            slot = i * 2 + zz
            term = jnp.dot(
                ntx[slot].reshape(768, 256), gx[slot, :, :, cols].reshape(256, 256), preferred_element_type=F32
            )
            value = term if value is None else value + term
        return value

    gq_own.wait()
    gq_core.wait_recv()
    for copy in na:
        copy.wait_recv()

    def first(i, _):
        cols = pl.ds(pl.multiple_of(i * 256, 256), 256)
        g[:, cols] = product(zh, cols)
        return 0

    lax.fori_loop(0, 6, first, 0)

    gl_own.wait()
    gl_core.wait_recv()
    gp_own.wait()
    h_own.wait()
    for copy in gl_fwd + gp_copies + h_copies:
        copy.wait_recv()
    d_copies = []
    for j, d in enumerate((2, 1, 3, 0)):
        to = lax.rem(x + d, 4)
        cols = pl.ds(pl.multiple_of(to * 384, 128), 384)
        xs[j, 0:448, :] = jnp.dot(
            hr[...].reshape(448, 1024), gla[:, :, cols].reshape(1024, 384), preferred_element_type=F32
        )
        total = gpa[0, :, cols]
        for i in range(1, 8):
            total = total + gpa[i, :, cols]
        xs[j, 448:456, :] = total
        if d:
            d_copies.append(send(xs.at[j], xr.at[j], d_s.at[j], d_r.at[j], device(x + d, y, z, c)))
    sends += d_copies

    for copy in nb:
        copy.wait_recv()
    u_copies = {}
    for n in range(3):

        def second(i, _):
            cols = pl.ds(pl.multiple_of(n * 512 + i * 256, 256), 256)
            g[:, cols] = g[:, cols] + product(1 - zh, cols)
            return 0

        lax.fori_loop(0, 2, second, 0)
        cols = pl.ds(n * 512, 512)
        for j, d in enumerate((2, 1, 3)):
            ty = lax.rem(y + d, 4)
            for k in range(4):
                rows = pl.ds(pl.multiple_of((k * 4 + ty) * 48, 16), 48)
                us[n, j, k] = g[rows, cols].astype(BF16)
            u_copies[n, j] = send(us.at[n, j], ur.at[n, j], u_s.at[n, j], u_r.at[n, j], device(x, y + d, z, c))
    sends += list(u_copies.values())

    for copy in d_copies:
        copy.wait_recv()
    for a in range(2):
        for b in range(4):
            rows, cols = slice(b * 112, b * 112 + 112), slice(a * 192, a * 192 + 192)
            total, tail = xs[3, rows, cols], xs[3, 448:456, cols]
            for j in range(3):
                total = total + xr[j, rows, cols]
                tail = tail + xr[j, 448:456, cols]
            zs[a * 4 + b, 0:112, :] = total
            zs[a * 4 + b, 112:120, :] = tail
    e_copies = [
        send(zs.at[lax.rem(z + d, 8)], zr.at[d - 1], e_s.at[d - 1], e_r.at[d - 1], device(x, y, z + d, c))
        for d in (4, 3, 5, 2, 6, 1, 7)
    ]
    sends += e_copies

    v_copies = {}
    for n in range(3):
        cols = pl.ds(n * 512, 512)
        for j in range(3):
            u_copies[n, j].wait_recv()
        for k in range(4):
            rows = pl.ds(pl.multiple_of((k * 4 + y) * 48, 16), 48)
            total = g[rows, cols]
            for j in range(3):
                total = total + ur[n, j, k].astype(F32)
            g[rows, cols] = total
            vs[n, k] = total.astype(BF16)
        for d in (2, 1, 3):
            to = lax.rem(zl + d, 4)
            v_copies[n, d] = send(
                vs.at[n, to], vr.at[n, d - 1], v_s.at[n, d - 1], v_r.at[n, d - 1], device(x, y, zh * 4 + to, c)
            )
    sends += list(v_copies.values())

    for copy in e_copies:
        copy.wait_recv()
    total = zs[z]
    for j in range(7):
        total = total + zr[j]
    gd_out[...] = total[0:112]
    gg_out[...] = total[112:113]
    my_rows = pl.ds(pl.multiple_of((zl * 4 + y) * 48, 16), 48)
    for n in range(3):
        cols = pl.ds(n * 512, 512)
        for d in (1, 2, 3):
            v_copies[n, d].wait_recv()
        total = g[my_rows, cols]
        for j in range(3):
            total = total + vr[n, j].astype(F32)
        gu_out[:, cols] = total
    for copy in sends:
        copy.wait_send()


VMEM = pl.BlockSpec(memory_space=pltpu.VMEM)
ANY = pl.BlockSpec(memory_space=pl.ANY)


def dma(*shape):
    return pltpu.SemaphoreType.DMA(shape) if shape else pltpu.SemaphoreType.DMA


def pairs(*shapes):
    return [dma(*shape) for shape in shapes for _ in range(2)]


def run_front(hidden, w_down, norm_gain, w_up, grad_query):
    return pl.pallas_call(
        front,
        out_shape=(
            jax.ShapeDtypeStruct((1536, 128), BF16),
            jax.ShapeDtypeStruct((128, 1536), BF16),
            jax.ShapeDtypeStruct((8, 1536), F32),
            jax.ShapeDtypeStruct((3584, 128), BF16),
        ),
        in_specs=[VMEM, ANY, VMEM, VMEM, VMEM],
        out_specs=(VMEM, VMEM, VMEM, VMEM),
        scratch_shapes=[
            pltpu.VMEM((2, 128, 1792), BF16),
            pltpu.VMEM((4, SUB, 192), BF16),
            pltpu.VMEM((8, 1, 192), F32),
            pltpu.VMEM((2, 1792, 768), BF16),
            pltpu.VMEM((3, 256, 1536), BF16),
            pltpu.VMEM((3, 256, 1536), BF16),
            pltpu.VMEM((256, 1536), F32),
            pltpu.VMEM((128, 1536), F32),
            pltpu.VMEM((128, 1536), F32),
            pltpu.VMEM((2, 2, 128, 768), F32),
            pltpu.VMEM((2, 128, 768), F32),
            pltpu.VMEM((128, 1536), F32),
            dma(3),
        ]
        + pairs((3,), (7,), (), (3, 2), (), (4,), (3,), (8,), (8,), (8,), ()),
        compiler_params=pltpu.CompilerParams(
            collective_id=0, has_side_effects=True, vmem_limit_bytes=56 * 2**20
        ),
    )(hidden, w_down, norm_gain.reshape(1, 192), w_up, grad_query)


def run_back(normed, grad_latent, gain_part, hidden, grad_query):
    return pl.pallas_call(
        back,
        out_shape=(
            jax.ShapeDtypeStruct((112, 192), F32),
            jax.ShapeDtypeStruct((48, 1536), F32),
            jax.ShapeDtypeStruct((1, 192), F32),
        ),
        in_specs=[VMEM, VMEM, VMEM, VMEM, ANY],
        out_specs=(VMEM, VMEM, VMEM),
        scratch_shapes=[
            pltpu.VMEM((8, 16, 48, 256), BF16),
            pltpu.VMEM((8, 2, 128, 1536), BF16),
            pltpu.VMEM((768, 1536), F32),
            pltpu.VMEM((4, SUB, 1024), BF16),
            pltpu.VMEM((8, 128, 1536), BF16),
            pltpu.VMEM((8, 8, 1536), F32),
            pltpu.VMEM((4, 456, 384), F32),
            pltpu.VMEM((3, 456, 384), F32),
            pltpu.VMEM((8, 120, 192), F32),
            pltpu.VMEM((7, 120, 192), F32),
            pltpu.VMEM((3, 3, 4, 48, 512), BF16),
            pltpu.VMEM((3, 3, 4, 48, 512), BF16),
            pltpu.VMEM((3, 4, 48, 512), BF16),
            pltpu.VMEM((3, 3, 48, 512), BF16),
            dma(5),
        ]
        + pairs((2,), (7,), (3,), (4,), (7,), (), (3,), (3,), (3,), (7,), (3, 3), (3, 3)),
        compiler_params=pltpu.CompilerParams(
            collective_id=1, has_side_effects=True, vmem_limit_bytes=56 * 2**20
        ),
    )(
        normed.reshape(16, 2, 48, 128),
        grad_latent,
        gain_part,
        hidden.reshape(4, 4, 2, SUB, 128),
        grad_query.reshape(8, 128, 1536),
    )


def local(hidden, w_down, norm_gain, w_up, grad_query):
    normed, grad_latent, gain_part, turned = run_front(hidden, w_down, norm_gain, w_up, grad_query)
    grad_down, grad_up, grad_gain = run_back(normed, grad_latent, gain_part, turned, grad_query)
    return grad_down, grad_up, grad_gain.reshape(192)


def solution(mesh):
    placed = (P(("dp", "st"), None), P(None, "st"), P("st"), P(None, "st"), P("dp", "st"))
    return jax.shard_map(
        local,
        mesh=mesh,
        in_specs=placed,
        out_specs=(P("dp", "st"), P("dp", "st"), P("st")),
        check_vma=False,
    )
```

```python
import functools

import jax
import jax.numpy as jnp
from jax import lax
from jax.experimental import pallas as pl
from jax.experimental.pallas import tpu as pltpu
from jax.sharding import PartitionSpec as P

L = 1536
MESH = pl.DeviceIdType.MESH
F32 = jnp.float32
BF16 = jnp.bfloat16
SUB = 112


def coordinates():
    dp = lax.axis_index("dp")
    st = lax.axis_index("st")
    zl, y, c = dp // 8, lax.rem(dp // 2, 4), lax.rem(dp, 2)
    x, zh = st // 2, lax.rem(st, 2)
    return x, y, zh * 4 + zl, c


def device(x, y, z, c):
    x, y, z, c = lax.rem(x + 8, 4), lax.rem(y + 8, 4), lax.rem(z + 16, 8), lax.rem(c + 2, 2)
    return ((lax.rem(z, 4) * 4 + y) * 2 + c, x * 2 + z // 4)


def send(src, dst, send_sem, recv_sem, to):
    copy = pltpu.make_async_remote_copy(
        src_ref=src, dst_ref=dst, send_sem=send_sem, recv_sem=recv_sem, device_id=to, device_id_type=MESH
    )
    copy.start()
    return copy


def whole(
    hid, wdt, gain, wup_hbm, gq, gd_out, gu_out, gg_out,
    wup, gx, wt, hk, xb, gb, w, snd, rcv, own, zs, zr, lp, lx, nat, ht,
    nt, nts, ntx, gla, gpa, hr, g, xs, xf, xo, xr, xfr, xg, xgr, ea, ear, eb, ebr, us, ur, vs, vr,
    loc_sem, x_s, x_r, g_s, g_r, h_s, h_r, n_s, n_r, q_s, q_r,
    za_s, za_r, zb_s, zb_r, yp_s, yp_r, ym_s, ym_r, yf_s, yf_r, l_s, l_r,
    c_s, c_r, t_s, t_r, glp_s, glp_r, glm_s, glm_r, glf_s, glf_r, glc_s, glc_r, gp_s, gp_r,
    z4_s, z4_r, np_s, np_r, nm_s, nm_r, nf_s, nf_r, d_s, d_r, dg_s, dg_r, e_s, e_r, u_s, u_r, v_s, v_r,
):
    x, y, z, c = coordinates()
    zh, zl = z // 4, lax.rem(z, 4)
    st = x * 2 + zh
    mine = y * 2 + c
    yc = [(dy, dc) for dy in (0, 1, 2, 3) for dc in (0, 1) if (dy, dc) != (0, 0)]
    s = 1 - 2 * c
    core_peer = device(x, y, z, c + 1)
    z4_peer = device(x, y, z + 4, c)
    up_x, down_x = device(x + 1, y, z, c), device(x - 1, y, z, c)
    up_y, down_y = device(x, y + 1, z, c), device(x, y - 1, z, c)
    up_z, down_z = device(x, y, z + s, c), device(x, y, z - s, c)
    peers = (
        [device(x + d, y, z, c) for d in (1, 2, 3)] + [up_y, down_y, up_z, down_z, z4_peer, core_peer]
    )
    barrier = pltpu.get_barrier_semaphore()
    for peer in peers:
        pl.semaphore_signal(barrier, inc=1, device_id=peer, device_id_type=MESH)
    loads = [
        pltpu.make_async_copy(gq, gx.at[:, c], loc_sem.at[0]),
        pltpu.make_async_copy(wup_hbm, wup, loc_sem.at[1]),
        pltpu.make_async_copy(hid.at[:, pl.ds(pl.multiple_of(c * 1792, 128), 1792)], hk.at[c], loc_sem.at[2]),
        pltpu.make_async_copy(gain, gb.at[zh, x], loc_sem.at[3]),
    ]
    for load in loads:
        load.start()
    row = (c * 16 + y * 4 + zl) * SUB
    base = jnp.minimum(row // 128, 26) * 128
    wt[...] = wdt[:, pl.ds(pl.multiple_of(base, 128), 256)].astype(F32).T.astype(BF16)
    piece = wt.at[pl.ds(pl.multiple_of(row - base, 16), SUB)]
    my_piece = pltpu.make_async_copy(piece, xb.at[x], loc_sem.at[4])
    my_piece.start()
    sends = []

    def cotangent(owner, store):
        def tile(i, _):
            cols = pl.ds(pl.multiple_of(i * 256, 256), 256)
            store(
                cols,
                lax.dot_general(
                    gx[pl.ds(owner * 2, 2), c].reshape(256, 1536),
                    wup[cols, :],
                    (((1,), (1,)), ((), ())),
                    preferred_element_type=F32,
                ),
            )
            return 0

        lax.fori_loop(0, 6, tile, 0)

    far = pl.ds(pl.multiple_of((1 - zh) * 128, 128), 128)
    near = pl.ds(pl.multiple_of(zh * 128, 128), 128)
    n_copies = {}

    def partial_for(j, d):
        def store(cols, value):
            snd[j, :, cols] = value.astype(BF16)

        cotangent(lax.rem(x + d, 4), store)

    def send_partial(j, d, h, rows):
        n_copies[j, h] = send(
            snd.at[j, rows], rcv.at[j, rows], n_s.at[j, h], n_r.at[j, h], device(x + d, y, z, c)
        )

    loads[0].wait()
    loads[1].wait()
    partial_for(0, 2)
    pl.semaphore_wait(barrier, len(peers))

    x_copies = [
        send(piece, xb.at[x], x_s.at[d - 1], x_r.at[d - 1], device(x + d, y, z, c)) for d in (2, 1, 3)
    ]
    send_partial(0, 2, 0, far)
    other_k = hid.at[:, pl.ds(pl.multiple_of((1 - c) * 1792, 128), 1792)]
    h_copy = send(other_k, hk.at[c], h_s, h_r, core_peer)
    g_copies = [
        send(gain, gb.at[zh, x], g_s.at[i], g_r.at[i], device(x + d, y, z, c)) for i, d in enumerate((2, 1, 3))
    ]
    gq_core = send(gq, gx.at[:, c], c_s.at[1], c_r.at[1], core_peer)
    sends += x_copies + [h_copy, gq_core] + g_copies

    partial_for(1, 1)
    send_partial(1, 1, 0, far)
    my_piece.wait()
    for copy in x_copies:
        copy.wait_recv()
    loads[3].wait()
    for copy in g_copies:
        copy.wait_recv()
    g_across = send(gb.at[zh], gb.at[zh], g_s.at[3], g_r.at[3], z4_peer)
    sends += [g_across]

    def unit(zz, yy):
        zz, yy = lax.rem(zz + 16, 8), lax.rem(yy + 8, 4)
        rows = pl.multiple_of((yy * 4 + lax.rem(zz, 4)) * SUB, 16)
        return w.at[zz // 4, pl.ds(rows, SUB)]

    my_rows = pl.ds(pl.multiple_of((y * 4 + zl) * SUB, 16), SUB)
    for i in range(4):
        w[zh, my_rows, i * 192 : (i + 1) * 192] = xb[i]

    owners = [z, z - s, z + s, z - 2 * s, z + 2 * s, z - 3 * s, z + 3 * s, z - 4 * s]
    za, zb, yp, ym, yf = {}, {}, {}, {}, {}

    def pass_on(k):
        here = unit(owners[k], y)
        if k == 0 or (k % 2 == 1 and k < 7):
            i = (k + 1) // 2
            za[i] = send(here, here, za_s.at[i], za_r.at[i], up_z)
        if k == 0 or (k % 2 == 0 and k < 6):
            i = k // 2
            zb[i] = send(here, here, zb_s.at[i], zb_r.at[i], down_z)
        yp[k] = send(here, here, yp_s.at[k], yp_r.at[k], up_y)
        ym[k] = send(here, here, ym_s.at[k], ym_r.at[k], down_y)

    def forward(k):
        yp[k].wait_recv()
        ym[k].wait_recv()
        if k % 2 == 0:
            there = unit(owners[k], y - 1)
            yf[k] = send(there, there, yf_s.at[k], yf_r.at[k], up_y)
        else:
            there = unit(owners[k], y + 1)
            yf[k] = send(there, there, yf_s.at[k], yf_r.at[k], down_y)

    pass_on(0)
    partial_for(2, 3)
    send_partial(2, 3, 0, far)
    def keep(cols, value):
        own[:, cols] = value

    za[0].wait_recv()
    pass_on(1)
    zb[0].wait_recv()
    pass_on(2)
    cotangent(x, keep)
    forward(0)
    for j, d in enumerate((2, 1, 3)):
        n_copies[j, 0].wait_send()
        send_partial(j, d, 1, near)
    za[1].wait_recv()
    pass_on(3)
    zb[1].wait_recv()
    pass_on(4)

    def turn(i, _):
        cols = pl.ds(pl.multiple_of(i * 896, 128), 896)
        ht[i] = hid[:, cols].astype(F32).T.astype(BF16).reshape(4, 2, SUB, 128)
        return 0

    forward(1)
    for j in range(3):
        n_copies[j, 0].wait_recv()
    total = own[far, :]
    for j in range(3):
        total = total + rcv[j, far, :].astype(F32)
    zs[...] = total.astype(BF16)
    q_copy = send(zs, zr, q_s, q_r, z4_peer)
    za[2].wait_recv()
    pass_on(5)
    zb[2].wait_recv()
    pass_on(6)
    forward(2)
    lax.fori_loop(0, 4, turn, 0)
    forward(3)
    za[3].wait_recv()
    pass_on(7)
    forward(4)
    forward(5)
    forward(6)
    forward(7)
    lanes_me = pl.ds(pl.multiple_of(mine * 128, 128), 128)
    t_copies = []
    for i, (dy, dc) in enumerate(yc):
        ty, tc = lax.rem(y + dy, 4), lax.rem(c + dc, 2)
        t_copies.append(
            send(ht.at[:, ty, tc], hr.at[:, :, lanes_me], t_s.at[i], t_r.at[i], device(x, y + dy, z, c + dc))
        )
    t_own = pltpu.make_async_copy(ht.at[:, y, c], hr.at[:, :, lanes_me], loc_sem.at[5])
    t_own.start()
    sends += t_copies
    for k in range(8):
        yf[k].wait_recv()
    h_copy.wait_recv()
    loads[2].wait()

    for half in range(2):

        def tile(i, _):
            cols = pl.ds(pl.multiple_of(i * 256, 256), 256)
            value = jnp.dot(hk[...].reshape(256, 1792), w[half, :, cols], preferred_element_type=F32)
            lp[:, half, :, cols] = value.reshape(2, 128, 256)
            return 0

        lax.fori_loop(0, 3, tile, 0)
    l_copy = send(lp.at[1 - c], lx, l_s, l_r, core_peer)

    g_across.wait_recv()
    for j in range(3):
        n_copies[j, 1].wait_recv()
    q_copy.wait_recv()
    total = own[near, :] + zr[...].astype(F32)
    for j in range(3):
        total = total + rcv[j, near, :].astype(F32)
    own[0:128, :] = total
    for i in range(8):
        gpa[mine, :, i * 192 : (i + 1) * 192] = gb[i % 2, i // 2]
    l_copy.wait_recv()
    for half in range(2):
        for i in range(4):
            piece_cols = pl.ds(i * 192, 192)
            at = i * 384 + half * 192
            nat[:, at : at + 192] = lp[c, half, :, piece_cols] + lx[half, :, piece_cols]
    latent = nat[...]
    inverse = lax.rsqrt(jnp.sum(latent * latent, axis=1, keepdims=True) / L + 1e-06)
    for i in range(12):
        cols = pl.ds(i * 128, 128)
        nt[cols, :] = (nat[:, cols] * inverse * gpa[mine, :, cols]).T.astype(BF16)
    lanes_c = pl.ds(pl.multiple_of(c * 128, 128), 128)
    for i in range(16):
        nts[i] = nt[pl.ds(pl.multiple_of(i * 96 + (1 - c) * 48, 16), 48), :]
    nt_core = send(nts, ntx.at[st, :, :, lanes_c], c_s.at[0], c_r.at[0], core_peer)
    for i in range(16):
        ntx[st, i, :, lanes_c] = nt[pl.ds(pl.multiple_of(i * 96 + c * 48, 16), 48), :]
    inner = jnp.sum(gpa[mine] * own[0:128, :] * nat[...], axis=1, keepdims=True)
    factor = inverse**3 * inner / L
    for i in range(12):
        cols = pl.ds(i * 128, 128)
        lat, cot = nat[:, cols], own[0:128, cols]
        value = inverse * gpa[mine, :, cols] * cot - lat * factor
        high = value.astype(BF16)
        gla[0, mine, :, cols] = high
        gla[1, mine, :, cols] = (value - high.astype(F32)).astype(BF16)
        gpa[mine, :, cols] = jnp.sum(cot * lat * inverse, axis=0, keepdims=True)

    mine_gl = [gla.at[v, mine] for v in range(2)]
    nt_core.wait_recv()
    glp = [send(mine_gl[0], mine_gl[0], glp_s.at[0], glp_r.at[0], up_y)]
    glm = [send(mine_gl[0], mine_gl[0], glm_s.at[0], glm_r.at[0], down_y)]

    def part(slot, h):
        return ntx.at[slot, pl.ds(h * 8, 8)]

    z4 = [send(part(st, h), part(st, h), z4_s.at[h], z4_r.at[h], z4_peer) for h in range(2)]
    np_, nm, nf = {}, {}, {}

    def spread(a, slot, order):
        for up, h in order:
            there = part(slot, h)
            if up:
                np_[a, h] = send(there, there, np_s.at[a, h], np_r.at[a, h], up_x)
            else:
                nm[a, h] = send(there, there, nm_s.at[a, h], nm_r.at[a, h], down_x)

    def relay(a, side):
        np_[a, 0].wait_recv()
        there = part(lax.rem(x + 3, 4) * 2 + side, 0)
        nf[a, 0] = send(there, there, nf_s.at[a, 0], nf_r.at[a, 0], up_x)
        nm[a, 1].wait_recv()
        there = part(lax.rem(x + 1, 4) * 2 + side, 1)
        nf[a, 1] = send(there, there, nf_s.at[a, 1], nf_r.at[a, 1], down_x)

    spread(0, st, ((True, 0), (False, 1), (False, 0), (True, 1)))
    glp.append(send(mine_gl[1], mine_gl[1], glp_s.at[1], glp_r.at[1], up_y))
    glm.append(send(mine_gl[1], mine_gl[1], glm_s.at[1], glm_r.at[1], down_y))
    gp_copies = [
        send(gpa.at[mine], gpa.at[mine], gp_s.at[i], gp_r.at[i], device(x, y + dy, z, c + dc))
        for i, (dy, dc) in enumerate(yc)
    ]
    glc = [send(mine_gl[v], mine_gl[v], glc_s.at[0, v], glc_r.at[0, v], core_peer) for v in range(2)]
    relay(0, zh)

    def to_core(v, i, dy):
        slot = gla.at[v, lax.rem(y + dy, 4) * 2 + c]
        glc.append(send(slot, slot, glc_s.at[i, v], glc_r.at[i, v], core_peer))
        return slot

    glp[0].wait_recv()
    slot = to_core(0, 1, 3)
    glf = [send(slot, slot, glf_s.at[0], glf_r.at[0], up_y)]
    glm[0].wait_recv()
    to_core(0, 2, 1)
    side = 1 - zh
    other = x * 2 + side
    z4[0].wait_recv()
    spread(1, other, ((True, 0), (False, 0)))

    def product(zz, cols):
        value = None
        for i in range(4):
            slot = i * 2 + zz
            term = jnp.dot(
                ntx[slot].reshape(768, 256), gx[slot, :, :, cols].reshape(256, 256), preferred_element_type=F32
            )
            value = term if value is None else value + term
        return value

    gq_core.wait_recv()
    np_[0, 1].wait_recv()
    nm[0, 0].wait_recv()
    nf[0, 0].wait_recv()
    nf[0, 1].wait_recv()

    def first(i, _):
        cols = pl.ds(pl.multiple_of(i * 256, 256), 256)
        g[:, cols] = product(zh, cols)
        return 0

    lax.fori_loop(0, 3, first, 0)
    z4[1].wait_recv()
    spread(1, other, ((False, 1), (True, 1)))
    glm[1].wait_recv()
    slot = to_core(1, 2, 1)
    glf.append(send(slot, slot, glf_s.at[1], glf_r.at[1], down_y))
    glp[1].wait_recv()
    to_core(1, 1, 3)
    lax.fori_loop(3, 6, first, 0)
    relay(1, side)
    glf[0].wait_recv()
    to_core(0, 3, 2)
    glf[1].wait_recv()
    to_core(1, 3, 2)
    sends += z4 + glp + glm + glf + glc + gp_copies + [nt_core]

    np_[1, 1].wait_recv()
    nm[1, 0].wait_recv()
    nf[1, 0].wait_recv()
    nf[1, 1].wait_recv()
    sends += list(np_.values()) + list(nm.values()) + list(nf.values())
    u_copies = {}
    for n in range(3):

        def second(i, _):
            cols = pl.ds(pl.multiple_of(n * 512 + i * 256, 256), 256)
            g[:, cols] = g[:, cols] + product(1 - zh, cols)
            return 0

        lax.fori_loop(0, 2, second, 0)
        cols = pl.ds(n * 512, 512)
        for j, d in enumerate((2, 1, 3)):
            ty = lax.rem(y + d, 4)
            for k in range(4):
                rows = pl.ds(pl.multiple_of((k * 4 + ty) * 48, 16), 48)
                us[n, j, k] = g[rows, cols].astype(BF16)
            u_copies[n, j] = send(us.at[n, j], ur.at[n, j], u_s.at[n, j], u_r.at[n, j], device(x, y + d, z, c))
    sends += list(u_copies.values())

    t_own.wait()
    for copy in glc + gp_copies + t_copies:
        copy.wait_recv()
    d_copies, dg_copies = {}, []
    split = (pl.ds(0, 64), pl.ds(64, 48))

    def outgoing(j):
        return xs if j == 0 else xf.at[j - 1]

    def arrived(j):
        return xr if j == 0 else xfr.at[j - 1]

    def send_down(j, d, h):
        d_copies[j, h] = send(
            outgoing(j).at[:, split[h]], arrived(j).at[:, split[h]],
            d_s.at[j, h], d_r.at[j, h], device(x + d, y, z, c),
        )

    for j, d in enumerate((2, 1, 3, 0)):
        to = lax.rem(x + d, 4)
        cols = pl.ds(pl.multiple_of(to * 384, 128), 384)
        rows = hr[...].reshape(448, 1024)
        value = jnp.dot(rows, gla[0, :, :, cols].reshape(1024, 384), preferred_element_type=F32) + jnp.dot(
            rows, gla[1, :, :, cols].reshape(1024, 384), preferred_element_type=F32
        )
        value = value.reshape(4, SUB, 384)
        total = gpa[0, :, cols]
        for i in range(1, 8):
            total = total + gpa[i, :, cols]
        xg[j] = jnp.broadcast_to(total, (8, 384))
        if d:
            outgoing(j)[...] = value.astype(outgoing(j).dtype)
            send_down(j, d, 0)
            dg_copies.append(send(xg.at[j], xgr.at[j], dg_s.at[j], dg_r.at[j], device(x + d, y, z, c)))
        else:
            xo[...] = value
    for j, d in enumerate((2, 1, 3)):
        send_down(j, d, 1)
    sends += list(d_copies.values()) + dg_copies

    v_copies = {}

    def narrow(n):
        cols = pl.ds(n * 512, 512)
        for j in range(3):
            u_copies[n, j].wait_recv()
        for k in range(4):
            rows = pl.ds(pl.multiple_of((k * 4 + y) * 48, 16), 48)
            total = g[rows, cols]
            for j in range(3):
                total = total + ur[n, j, k].astype(F32)
            g[rows, cols] = total
            vs[n, k] = total.astype(BF16)
        for d in (2, 1, 3):
            to = lax.rem(zl + d, 4)
            v_copies[n, d] = send(
                vs.at[n, to], vr.at[n, d - 1], v_s.at[n, d - 1], v_r.at[n, d - 1], device(x, y, zh * 4 + to, c)
            )

    e_copies = {}

    def deliver(h, buffer, landing):
        begin, size = ((0, 64), (64, 48))[h]
        for j in range(3):
            d_copies[j, h].wait_recv()
        for b in range(4):
            total = xo[b, begin : begin + size, :]
            for j in range(3):
                total = total + arrived(j)[b, begin : begin + size, :].astype(F32)
            xo[b, begin : begin + size, :] = total
            for a in range(2):
                at, mid = a * 192, begin + size // 2
                i = a * 4 + b
                buffer[i, 0:size, :] = xo[b, begin : begin + size, at : at + 128]
                buffer[i, size : size + size // 2, 0:64] = xo[b, begin:mid, at + 128 : at + 192]
                buffer[i, size : size + size // 2, 64:128] = xo[b, mid : begin + size, at + 128 : at + 192]
        if h:
            for copy in dg_copies:
                copy.wait_recv()
            total = xg[3]
            for j in range(3):
                total = total + xgr[j]
            xg[3] = total
            for a in range(2):
                for b in range(4):
                    buffer[a * 4 + b, 72:80, :] = jnp.zeros((8, 128), F32)
                    buffer[a * 4 + b, 72:73, :] = xg[3, 0:1, a * 192 : a * 192 + 128]
                    buffer[a * 4 + b, 73:74, 0:64] = xg[3, 0:1, a * 192 + 128 : a * 192 + 192]
        for d in (4, 3, 5, 2, 6, 1, 7):
            e_copies[h, d] = send(
                buffer.at[lax.rem(z + d, 8)], landing.at[d - 1],
                e_s.at[h, d - 1], e_r.at[h, d - 1], device(x, y, z + d, c),
            )

    narrow(0)
    deliver(0, ea, ear)
    narrow(1)
    deliver(1, eb, ebr)
    narrow(2)
    sends += list(v_copies.values()) + list(e_copies.values())

    for h, (buffer, landing) in enumerate(((ea, ear), (eb, ebr))):
        begin, size = ((0, 64), (64, 48))[h]
        for d in range(1, 8):
            e_copies[h, d].wait_recv()
        total = buffer[z]
        for j in range(7):
            total = total + landing[j]
        half = size // 2
        gd_out[begin : begin + size, 0:128] = total[0:size]
        gd_out[begin : begin + half, 128:192] = total[size : size + half, 0:64]
        gd_out[begin + half : begin + size, 128:192] = total[size : size + half, 64:128]
        if h:
            gg_out[:, 0:128] = total[72:73]
            gg_out[:, 128:192] = total[73:74, 0:64]
    my_rows = pl.ds(pl.multiple_of((zl * 4 + y) * 48, 16), 48)
    for n in range(3):
        cols = pl.ds(n * 512, 512)
        for d in (1, 2, 3):
            v_copies[n, d].wait_recv()
        total = g[my_rows, cols]
        for j in range(3):
            total = total + vr[n, j].astype(F32)
        gu_out[:, cols] = total
    sends += [n_copies[j, 1] for j in range(3)] + [q_copy, l_copy]
    for group in (za, zb, yp, ym, yf):
        sends += list(group.values())
    for copy in sends:
        copy.wait_send()


VMEM = pl.BlockSpec(memory_space=pltpu.VMEM)
ANY = pl.BlockSpec(memory_space=pl.ANY)


def dma(*shape):
    return pltpu.SemaphoreType.DMA(shape) if shape else pltpu.SemaphoreType.DMA


def pairs(*shapes):
    return [dma(*shape) for shape in shapes for _ in range(2)]


def local(hidden, w_down, norm_gain, w_up, grad_query):
    grad_down, grad_up, grad_gain = pl.pallas_call(
        whole,
        out_shape=(
            jax.ShapeDtypeStruct((112, 192), F32),
            jax.ShapeDtypeStruct((48, 1536), F32),
            jax.ShapeDtypeStruct((1, 192), F32),
        ),
        in_specs=[VMEM, VMEM, VMEM, ANY, ANY],
        out_specs=(VMEM, VMEM, VMEM),
        scratch_shapes=[
            pltpu.VMEM((1536, 1536), BF16),
            pltpu.VMEM((8, 2, 128, 1536), BF16),
            pltpu.VMEM((256, 192), BF16),
            pltpu.VMEM((2, 128, 1792), BF16),
            pltpu.VMEM((4, SUB, 192), BF16),
            pltpu.VMEM((2, 4, 1, 192), F32),
            pltpu.VMEM((2, 1792, 768), BF16),
            pltpu.VMEM((3, 256, 1536), BF16),
            pltpu.VMEM((3, 256, 1536), BF16),
            pltpu.VMEM((256, 1536), F32),
            pltpu.VMEM((128, 1536), BF16),
            pltpu.VMEM((128, 1536), BF16),
            pltpu.VMEM((2, 2, 128, 768), F32),
            pltpu.VMEM((2, 128, 768), F32),
            pltpu.VMEM((128, 1536), F32),
            pltpu.VMEM((4, 4, 2, SUB, 128), BF16),
            pltpu.VMEM((1536, 128), BF16),
            pltpu.VMEM((16, 48, 128), BF16),
            pltpu.VMEM((8, 16, 48, 256), BF16),
            pltpu.VMEM((2, 8, 128, 1536), BF16),
            pltpu.VMEM((8, 1, 1536), F32),
            pltpu.VMEM((4, SUB, 1024), BF16),
            pltpu.VMEM((768, 1536), F32),
            pltpu.VMEM((4, SUB, 384), BF16),
            pltpu.VMEM((2, 4, SUB, 384), F32),
            pltpu.VMEM((4, SUB, 384), F32),
            pltpu.VMEM((4, SUB, 384), BF16),
            pltpu.VMEM((2, 4, SUB, 384), F32),
            pltpu.VMEM((4, 8, 384), F32),
            pltpu.VMEM((3, 8, 384), F32),
            pltpu.VMEM((8, 96, 128), F32),
            pltpu.VMEM((7, 96, 128), F32),
            pltpu.VMEM((8, 80, 128), F32),
            pltpu.VMEM((7, 80, 128), F32),
            pltpu.VMEM((3, 3, 4, 48, 512), BF16),
            pltpu.VMEM((3, 3, 4, 48, 512), BF16),
            pltpu.VMEM((3, 4, 48, 512), BF16),
            pltpu.VMEM((3, 3, 48, 512), BF16),
            dma(6),
        ]
        + pairs((3,), (4,), (), (3, 2), (), (4,), (3,), (8,), (8,), (8,), ())
        + pairs((2,), (7,), (2,), (2,), (2,), (4, 2), (7,), (2,), (2, 2), (2, 2), (2, 2), (3, 2), (3,), (2, 7))
        + pairs((3, 3), (3, 3)),
        compiler_params=pltpu.CompilerParams(
            collective_id=0, has_side_effects=True, vmem_limit_bytes=62 * 2**20
        ),
    )(hidden, w_down.T, norm_gain.reshape(1, 192), w_up, grad_query.reshape(8, 128, 1536))
    return grad_down, grad_up, grad_gain.reshape(192)


def solution(mesh):
    placed = (P(("dp", "st"), None), P(None, "st"), P("st"), P(None, "st"), P("dp", "st"))
    return jax.shard_map(
        local,
        mesh=mesh,
        in_specs=placed,
        out_specs=(P("dp", "st"), P("dp", "st"), P("st")),
        check_vma=False,
    )
```

```python
import functools

import jax
import jax.numpy as jnp
from jax import lax
from jax.experimental import pallas as pl
from jax.experimental.pallas import tpu as pltpu
from jax.sharding import PartitionSpec as P

L = 1536
MESH = pl.DeviceIdType.MESH
F32 = jnp.float32
BF16 = jnp.bfloat16
SUB = 112
PARTS = ((0, 48), (48, 48), (96, 16))


def coordinates():
    dp = lax.axis_index("dp")
    st = lax.axis_index("st")
    zl, y, c = dp // 8, lax.rem(dp // 2, 4), lax.rem(dp, 2)
    x, zh = st // 2, lax.rem(st, 2)
    return x, y, zh * 4 + zl, c


def device(x, y, z, c):
    x, y, z, c = lax.rem(x + 8, 4), lax.rem(y + 8, 4), lax.rem(z + 16, 8), lax.rem(c + 2, 2)
    return ((lax.rem(z, 4) * 4 + y) * 2 + c, x * 2 + z // 4)


def send(src, dst, send_sem, recv_sem, to):
    copy = pltpu.make_async_remote_copy(
        src_ref=src, dst_ref=dst, send_sem=send_sem, recv_sem=recv_sem, device_id=to, device_id_type=MESH
    )
    copy.start()
    return copy


def whole(
    hid, wdt, gain, wup_hbm, gq, gd_out, gu_out, gg_out,
    hidv, wdv, wup, gx, wt, hk, xb, gb, w, snd, rcv, own, zs, zr, lp, lx, nat, ht,
    nt, nts, ntx, gla, gpa, hr, g, xs, xf, xo, xr, xfr, xg, xgr, ea, ear, eb, ebr, ec, ecr, us, ur, vs, vr,
    loc_sem, x_s, x_r, g_s, g_r, h_s, h_r, n_s, n_r, q_s, q_r,
    za_s, za_r, zb_s, zb_r, yp_s, yp_r, ym_s, ym_r, yf_s, yf_r, l_s, l_r,
    c_s, c_r, t_s, t_r, glp_s, glp_r, glm_s, glm_r, glf_s, glf_r, glc_s, glc_r, gp_s, gp_r,
    z4_s, z4_r, np_s, np_r, nm_s, nm_r, nf_s, nf_r, d_s, d_r, dg_s, dg_r, e_s, e_r, u_s, u_r, v_s, v_r,
):
    x, y, z, c = coordinates()
    zh, zl = z // 4, lax.rem(z, 4)
    st = x * 2 + zh
    mine = y * 2 + c
    yc = [(dy, dc) for dy in (0, 1, 2, 3) for dc in (0, 1) if (dy, dc) != (0, 0)]
    s = 1 - 2 * c
    core_peer = device(x, y, z, c + 1)
    z4_peer = device(x, y, z + 4, c)
    up_x, down_x = device(x + 1, y, z, c), device(x - 1, y, z, c)
    up_y, down_y = device(x, y + 1, z, c), device(x, y - 1, z, c)
    up_z, down_z = device(x, y, z + s, c), device(x, y, z - s, c)
    peers = (
        [device(x + d, y, z, c) for d in (1, 2, 3)] + [up_y, down_y, up_z, down_z, z4_peer, core_peer]
    )
    barrier = pltpu.get_barrier_semaphore()
    for peer in peers:
        pl.semaphore_signal(barrier, inc=1, device_id=peer, device_id_type=MESH)
    loads = [
        pltpu.make_async_copy(gq, gx.at[:, c], loc_sem.at[0]),
        pltpu.make_async_copy(wup_hbm, wup, loc_sem.at[1]),
        pltpu.make_async_copy(hid.at[:, pl.ds(pl.multiple_of(c * 1792, 128), 1792)], hk.at[c], loc_sem.at[2]),
        pltpu.make_async_copy(gain, gb.at[zh, x], loc_sem.at[3]),
        pltpu.make_async_copy(hid, hidv, loc_sem.at[6]),
    ]
    row = (c * 16 + y * 4 + zl) * SUB
    base = jnp.minimum(row // 128, 26) * 128
    window = pltpu.make_async_copy(wdt.at[:, pl.ds(pl.multiple_of(base, 128), 256)], wdv, loc_sem.at[7])
    window.start()
    loads[4].start()
    for load in loads[:4]:
        load.start()
    window.wait()
    wt[...] = wdv[...].astype(F32).T.astype(BF16)
    piece = wt.at[pl.ds(pl.multiple_of(row - base, 16), SUB)]
    my_piece = pltpu.make_async_copy(piece, xb.at[x], loc_sem.at[4])
    my_piece.start()
    sends = []

    def cotangent(owner, store):
        def tile(i, _):
            cols = pl.ds(pl.multiple_of(i * 256, 256), 256)
            store(
                cols,
                lax.dot_general(
                    gx[pl.ds(owner * 2, 2), c].reshape(256, 1536),
                    wup[cols, :],
                    (((1,), (1,)), ((), ())),
                    preferred_element_type=F32,
                ),
            )
            return 0

        lax.fori_loop(0, 6, tile, 0)

    far = pl.ds(pl.multiple_of((1 - zh) * 128, 128), 128)
    near = pl.ds(pl.multiple_of(zh * 128, 128), 128)
    n_copies = {}

    def partial_for(j, d):
        def store(cols, value):
            snd[j, :, cols] = value.astype(BF16)

        cotangent(lax.rem(x + d, 4), store)

    def keep(cols, value):
        own[:, cols] = value

    def send_partial(j, d, h, rows):
        n_copies[j, h] = send(
            snd.at[j, rows], rcv.at[j, rows], n_s.at[j, h], n_r.at[j, h], device(x + d, y, z, c)
        )

    def turn(i, _):
        cols = pl.ds(pl.multiple_of(i * 896, 128), 896)
        ht[i] = hidv[:, cols].astype(F32).T.astype(BF16).reshape(4, 2, SUB, 128)
        return 0

    loads[4].wait()
    lax.fori_loop(0, 4, turn, 0)
    loads[0].wait()
    loads[1].wait()
    partial_for(0, 2)
    partial_for(1, 1)
    pl.semaphore_wait(barrier, len(peers))

    x_copies = [
        send(piece, xb.at[x], x_s.at[d - 1], x_r.at[d - 1], device(x + d, y, z, c)) for d in (2, 1, 3)
    ]
    other_k = hid.at[:, pl.ds(pl.multiple_of((1 - c) * 1792, 128), 1792)]
    h_copy = send(other_k, hk.at[c], h_s, h_r, core_peer)
    g_copies = [
        send(gain, gb.at[zh, x], g_s.at[i], g_r.at[i], device(x + d, y, z, c)) for i, d in enumerate((2, 1, 3))
    ]
    gq_core = send(gq, gx.at[:, c], c_s.at[1], c_r.at[1], core_peer)
    sends += x_copies + [h_copy, gq_core] + g_copies

    partial_for(2, 3)
    my_piece.wait()
    for copy in x_copies:
        copy.wait_recv()
    loads[3].wait()
    for copy in g_copies:
        copy.wait_recv()
    g_across = send(gb.at[zh], gb.at[zh], g_s.at[3], g_r.at[3], z4_peer)
    sends += [g_across]

    def unit(zz, yy):
        zz, yy = lax.rem(zz + 16, 8), lax.rem(yy + 8, 4)
        rows = pl.multiple_of((yy * 4 + lax.rem(zz, 4)) * SUB, 16)
        return w.at[zz // 4, pl.ds(rows, SUB)]

    my_rows = pl.ds(pl.multiple_of((y * 4 + zl) * SUB, 16), SUB)
    for i in range(4):
        w[zh, my_rows, i * 192 : (i + 1) * 192] = xb[i]

    owners = [z, z - s, z + s, z - 2 * s, z + 2 * s, z - 3 * s, z + 3 * s, z - 4 * s]
    za, zb, yp, ym, yf = {}, {}, {}, {}, {}

    def pass_on(k):
        here = unit(owners[k], y)
        if k == 0 or (k % 2 == 1 and k < 7):
            i = (k + 1) // 2
            za[i] = send(here, here, za_s.at[i], za_r.at[i], up_z)
        if k == 0 or (k % 2 == 0 and k < 6):
            i = k // 2
            zb[i] = send(here, here, zb_s.at[i], zb_r.at[i], down_z)
        yp[k] = send(here, here, yp_s.at[k], yp_r.at[k], up_y)
        ym[k] = send(here, here, ym_s.at[k], ym_r.at[k], down_y)

    def forward(k):
        yp[k].wait_recv()
        ym[k].wait_recv()
        if k % 2 == 0:
            there = unit(owners[k], y - 1)
            yf[k] = send(there, there, yf_s.at[k], yf_r.at[k], up_y)
        else:
            there = unit(owners[k], y + 1)
            yf[k] = send(there, there, yf_s.at[k], yf_r.at[k], down_y)

    pass_on(0)
    for j, d in enumerate((2, 1, 3)):
        send_partial(j, d, 0, far)
    cotangent(x, keep)
    za[0].wait_recv()
    pass_on(1)
    zb[0].wait_recv()
    pass_on(2)
    forward(0)
    za[1].wait_recv()
    pass_on(3)
    zb[1].wait_recv()
    pass_on(4)

    forward(1)
    for j, d in enumerate((2, 1, 3)):
        n_copies[j, 0].wait_send()
        send_partial(j, d, 1, near)
    za[2].wait_recv()
    pass_on(5)
    zb[2].wait_recv()
    pass_on(6)
    forward(2)
    for j in range(3):
        n_copies[j, 0].wait_recv()
    total = own[far, :]
    for j in range(3):
        total = total + rcv[j, far, :].astype(F32)
    zs[...] = total.astype(BF16)
    q_copy = send(zs, zr, q_s, q_r, z4_peer)
    forward(3)
    za[3].wait_recv()
    pass_on(7)
    forward(4)
    forward(5)
    forward(6)
    forward(7)
    lanes_me = pl.ds(pl.multiple_of(mine * 128, 128), 128)
    t_copies = []
    for i, (dy, dc) in enumerate(yc):
        ty, tc = lax.rem(y + dy, 4), lax.rem(c + dc, 2)
        t_copies.append(
            send(ht.at[:, ty, tc], hr.at[:, :, lanes_me], t_s.at[i], t_r.at[i], device(x, y + dy, z, c + dc))
        )
    t_own = pltpu.make_async_copy(ht.at[:, y, c], hr.at[:, :, lanes_me], loc_sem.at[5])
    t_own.start()
    sends += t_copies
    for k in range(8):
        yf[k].wait_recv()
    h_copy.wait_recv()
    loads[2].wait()

    for half in range(2):

        def tile(i, _):
            cols = pl.ds(pl.multiple_of(i * 256, 256), 256)
            value = jnp.dot(hk[...].reshape(256, 1792), w[half, :, cols], preferred_element_type=F32)
            lp[:, half, :, cols] = value.reshape(2, 128, 256)
            return 0

        lax.fori_loop(0, 3, tile, 0)
    l_copy = send(lp.at[1 - c], lx, l_s, l_r, core_peer)

    g_across.wait_recv()
    for j in range(3):
        n_copies[j, 1].wait_recv()
    q_copy.wait_recv()
    total = own[near, :] + zr[...].astype(F32)
    for j in range(3):
        total = total + rcv[j, near, :].astype(F32)
    own[0:128, :] = total
    for i in range(8):
        gpa[mine, :, i * 192 : (i + 1) * 192] = gb[i % 2, i // 2]
    l_copy.wait_recv()
    for half in range(2):
        for i in range(4):
            piece_cols = pl.ds(i * 192, 192)
            at = i * 384 + half * 192
            nat[:, at : at + 192] = lp[c, half, :, piece_cols] + lx[half, :, piece_cols]
    latent = nat[...]
    inverse = lax.rsqrt(jnp.sum(latent * latent, axis=1, keepdims=True) / L + 1e-06)
    for i in range(12):
        cols = pl.ds(i * 128, 128)
        nt[cols, :] = (nat[:, cols] * inverse * gpa[mine, :, cols]).T.astype(BF16)
    lanes_c = pl.ds(pl.multiple_of(c * 128, 128), 128)
    for i in range(16):
        nts[i] = nt[pl.ds(pl.multiple_of(i * 96 + (1 - c) * 48, 16), 48), :]
    nt_core = send(nts, ntx.at[st, :, :, lanes_c], c_s.at[0], c_r.at[0], core_peer)
    for i in range(16):
        ntx[st, i, :, lanes_c] = nt[pl.ds(pl.multiple_of(i * 96 + c * 48, 16), 48), :]
    inner = jnp.sum(gpa[mine] * own[0:128, :] * nat[...], axis=1, keepdims=True)
    factor = inverse**3 * inner / L
    for i in range(12):
        cols = pl.ds(i * 128, 128)
        lat, cot = nat[:, cols], own[0:128, cols]
        value = inverse * gpa[mine, :, cols] * cot - lat * factor
        high = value.astype(BF16)
        gla[0, mine, :, cols] = high
        gla[1, mine, :, cols] = (value - high.astype(F32)).astype(BF16)
        gpa[mine, :, cols] = jnp.sum(cot * lat * inverse, axis=0, keepdims=True)

    mine_gl = [gla.at[v, mine] for v in range(2)]
    glp = [send(mine_gl[0], mine_gl[0], glp_s.at[0], glp_r.at[0], up_y)]
    glm = [send(mine_gl[0], mine_gl[0], glm_s.at[0], glm_r.at[0], down_y)]

    def part(slot, h):
        return ntx.at[slot, pl.ds(h * 8, 8)]

    nt_core.wait_recv()
    z4 = [send(part(st, h), part(st, h), z4_s.at[h], z4_r.at[h], z4_peer) for h in range(2)]
    np_, nm, nf = {}, {}, {}

    def spread(a, slot, order):
        for up, h in order:
            there = part(slot, h)
            if up:
                np_[a, h] = send(there, there, np_s.at[a, h], np_r.at[a, h], up_x)
            else:
                nm[a, h] = send(there, there, nm_s.at[a, h], nm_r.at[a, h], down_x)

    def relay(a, side):
        np_[a, 0].wait_recv()
        there = part(lax.rem(x + 3, 4) * 2 + side, 0)
        nf[a, 0] = send(there, there, nf_s.at[a, 0], nf_r.at[a, 0], up_x)
        nm[a, 1].wait_recv()
        there = part(lax.rem(x + 1, 4) * 2 + side, 1)
        nf[a, 1] = send(there, there, nf_s.at[a, 1], nf_r.at[a, 1], down_x)

    spread(0, st, ((True, 0), (False, 1), (False, 0), (True, 1)))
    glp.append(send(mine_gl[1], mine_gl[1], glp_s.at[1], glp_r.at[1], up_y))
    glm.append(send(mine_gl[1], mine_gl[1], glm_s.at[1], glm_r.at[1], down_y))
    gp_copies = [
        send(gpa.at[mine], gpa.at[mine], gp_s.at[i], gp_r.at[i], device(x, y + dy, z, c + dc))
        for i, (dy, dc) in enumerate(yc)
    ]
    glc = [send(mine_gl[v], mine_gl[v], glc_s.at[0, v], glc_r.at[0, v], core_peer) for v in range(2)]
    relay(0, zh)

    def to_core(v, i, dy):
        slot = gla.at[v, lax.rem(y + dy, 4) * 2 + c]
        glc.append(send(slot, slot, glc_s.at[i, v], glc_r.at[i, v], core_peer))
        return slot

    glp[0].wait_recv()
    slot = to_core(0, 1, 3)
    glf = [send(slot, slot, glf_s.at[0], glf_r.at[0], up_y)]
    glm[0].wait_recv()
    to_core(0, 2, 1)
    side = 1 - zh
    other = x * 2 + side
    z4[0].wait_recv()
    spread(1, other, ((True, 0), (False, 0)))

    def product(zz, cols):
        value = None
        for i in range(4):
            slot = i * 2 + zz
            term = jnp.dot(
                ntx[slot].reshape(768, 256), gx[slot, :, :, cols].reshape(256, 256), preferred_element_type=F32
            )
            value = term if value is None else value + term
        return value

    gq_core.wait_recv()
    np_[0, 1].wait_recv()
    nm[0, 0].wait_recv()
    nf[0, 0].wait_recv()
    nf[0, 1].wait_recv()

    def first(i, _):
        cols = pl.ds(pl.multiple_of(i * 256, 256), 256)
        g[:, cols] = product(zh, cols)
        return 0

    lax.fori_loop(0, 3, first, 0)
    z4[1].wait_recv()
    spread(1, other, ((False, 1), (True, 1)))
    glm[1].wait_recv()
    slot = to_core(1, 2, 1)
    glf.append(send(slot, slot, glf_s.at[1], glf_r.at[1], down_y))
    glp[1].wait_recv()
    to_core(1, 1, 3)
    lax.fori_loop(3, 6, first, 0)
    relay(1, side)
    glf[0].wait_recv()
    to_core(0, 3, 2)
    glf[1].wait_recv()
    to_core(1, 3, 2)
    sends += z4 + glp + glm + glf + glc + gp_copies + [nt_core]

    t_own.wait()
    for copy in glc + gp_copies + t_copies:
        copy.wait_recv()
    d_copies, dg_copies = {}, []
    split = [pl.ds(begin, size) for begin, size in PARTS]

    def outgoing(j):
        return xs if j == 0 else xf.at[j - 1]

    def arrived(j):
        return xr if j == 0 else xfr.at[j - 1]

    def send_down(j, d, h):
        d_copies[j, h] = send(
            outgoing(j).at[:, split[h]], arrived(j).at[:, split[h]],
            d_s.at[j, h], d_r.at[j, h], device(x + d, y, z, c),
        )

    for j, d in enumerate((2, 1, 3, 0)):
        to = lax.rem(x + d, 4)
        cols = pl.ds(pl.multiple_of(to * 384, 128), 384)
        rows = hr[...].reshape(448, 1024)
        value = jnp.dot(rows, gla[0, :, :, cols].reshape(1024, 384), preferred_element_type=F32) + jnp.dot(
            rows, gla[1, :, :, cols].reshape(1024, 384), preferred_element_type=F32
        )
        value = value.reshape(4, SUB, 384)
        total = gpa[0, :, cols]
        for i in range(1, 8):
            total = total + gpa[i, :, cols]
        xg[j] = jnp.broadcast_to(total, (8, 384))
        if d:
            outgoing(j)[...] = value.astype(outgoing(j).dtype)
            send_down(j, d, 0)
            dg_copies.append(send(xg.at[j], xgr.at[j], dg_s.at[j], dg_r.at[j], device(x + d, y, z, c)))
        else:
            xo[...] = value
    for h in (1, 2):
        for j, d in enumerate((2, 1, 3)):
            send_down(j, d, h)
    sends += list(d_copies.values()) + dg_copies

    np_[1, 1].wait_recv()
    nm[1, 0].wait_recv()
    nf[1, 0].wait_recv()
    nf[1, 1].wait_recv()
    sends += list(np_.values()) + list(nm.values()) + list(nf.values())
    u_copies = {}
    for n in range(3):

        def second(i, _):
            cols = pl.ds(pl.multiple_of(n * 512 + i * 256, 256), 256)
            g[:, cols] = g[:, cols] + product(1 - zh, cols)
            return 0

        lax.fori_loop(0, 2, second, 0)
        cols = pl.ds(n * 512, 512)
        for j, d in enumerate((2, 1, 3)):
            ty = lax.rem(y + d, 4)
            for k in range(4):
                rows = pl.ds(pl.multiple_of((k * 4 + ty) * 48, 16), 48)
                us[n, j, k] = g[rows, cols].astype(BF16)
            u_copies[n, j] = send(us.at[n, j], ur.at[n, j], u_s.at[n, j], u_r.at[n, j], device(x, y + d, z, c))
    sends += list(u_copies.values())

    v_copies = {}

    def narrow(n):
        cols = pl.ds(n * 512, 512)
        for j in range(3):
            u_copies[n, j].wait_recv()
        for k in range(4):
            rows = pl.ds(pl.multiple_of((k * 4 + y) * 48, 16), 48)
            total = g[rows, cols]
            for j in range(3):
                total = total + ur[n, j, k].astype(F32)
            g[rows, cols] = total
            vs[n, k] = total.astype(BF16)
        for d in (2, 1, 3):
            to = lax.rem(zl + d, 4)
            v_copies[n, d] = send(
                vs.at[n, to], vr.at[n, d - 1], v_s.at[n, d - 1], v_r.at[n, d - 1], device(x, y, zh * 4 + to, c)
            )

    e_copies = {}

    def deliver(h, buffer, landing):
        begin, size = PARTS[h]
        for j in range(3):
            d_copies[j, h].wait_recv()
        for b in range(4):
            total = xo[b, begin : begin + size, :]
            for j in range(3):
                total = total + arrived(j)[b, begin : begin + size, :].astype(F32)
            xo[b, begin : begin + size, :] = total
            for a in range(2):
                at, mid = a * 192, begin + size // 2
                i = a * 4 + b
                buffer[i, 0:size, :] = xo[b, begin : begin + size, at : at + 128]
                buffer[i, size : size + size // 2, 0:64] = xo[b, begin:mid, at + 128 : at + 192]
                buffer[i, size : size + size // 2, 64:128] = xo[b, mid : begin + size, at + 128 : at + 192]
        if h == 2:
            for copy in dg_copies:
                copy.wait_recv()
            total = xg[3]
            for j in range(3):
                total = total + xgr[j]
            xg[3] = total
            for a in range(2):
                for b in range(4):
                    buffer[a * 4 + b, 24:32, :] = jnp.zeros((8, 128), F32)
                    buffer[a * 4 + b, 24:25, :] = xg[3, 0:1, a * 192 : a * 192 + 128]
                    buffer[a * 4 + b, 25:26, 0:64] = xg[3, 0:1, a * 192 + 128 : a * 192 + 192]
        for d in (4, 3, 5, 2, 6, 1, 7):
            e_copies[h, d] = send(
                buffer.at[lax.rem(z + d, 8)], landing.at[d - 1],
                e_s.at[h, d - 1], e_r.at[h, d - 1], device(x, y, z + d, c),
            )

    deliver(0, ea, ear)
    narrow(0)
    narrow(1)
    deliver(1, eb, ebr)
    deliver(2, ec, ecr)
    narrow(2)
    sends += list(v_copies.values()) + list(e_copies.values())

    for h, (buffer, landing) in enumerate(((ea, ear), (eb, ebr), (ec, ecr))):
        begin, size = PARTS[h]
        for d in range(1, 8):
            e_copies[h, d].wait_recv()
        total = buffer[z]
        for j in range(7):
            total = total + landing[j]
        half = size // 2
        gd_out[begin : begin + size, 0:128] = total[0:size]
        gd_out[begin : begin + half, 128:192] = total[size : size + half, 0:64]
        gd_out[begin + half : begin + size, 128:192] = total[size : size + half, 64:128]
        if h == 2:
            gg_out[:, 0:128] = total[24:25]
            gg_out[:, 128:192] = total[25:26, 0:64]
    my_rows = pl.ds(pl.multiple_of((zl * 4 + y) * 48, 16), 48)
    for n in range(3):
        cols = pl.ds(n * 512, 512)
        for d in (1, 2, 3):
            v_copies[n, d].wait_recv()
        total = g[my_rows, cols]
        for j in range(3):
            total = total + vr[n, j].astype(F32)
        gu_out[:, cols] = total
    sends += [n_copies[j, 1] for j in range(3)] + [q_copy, l_copy]
    for group in (za, zb, yp, ym, yf):
        sends += list(group.values())
    for copy in sends:
        copy.wait_send()


VMEM = pl.BlockSpec(memory_space=pltpu.VMEM)
ANY = pl.BlockSpec(memory_space=pl.ANY)


def dma(*shape):
    return pltpu.SemaphoreType.DMA(shape) if shape else pltpu.SemaphoreType.DMA


def pairs(*shapes):
    return [dma(*shape) for shape in shapes for _ in range(2)]


def local(hidden, w_down, norm_gain, w_up, grad_query):
    grad_down, grad_up, grad_gain = pl.pallas_call(
        whole,
        out_shape=(
            jax.ShapeDtypeStruct((112, 192), F32),
            jax.ShapeDtypeStruct((48, 1536), F32),
            jax.ShapeDtypeStruct((1, 192), F32),
        ),
        in_specs=[ANY, ANY, VMEM, ANY, ANY],
        out_specs=(VMEM, VMEM, VMEM),
        scratch_shapes=[
            pltpu.VMEM((128, 3584), BF16),
            pltpu.VMEM((192, 256), BF16),
            pltpu.VMEM((1536, 1536), BF16),
            pltpu.VMEM((8, 2, 128, 1536), BF16),
            pltpu.VMEM((256, 192), BF16),
            pltpu.VMEM((2, 128, 1792), BF16),
            pltpu.VMEM((4, SUB, 192), BF16),
            pltpu.VMEM((2, 4, 1, 192), F32),
            pltpu.VMEM((2, 1792, 768), BF16),
            pltpu.VMEM((3, 256, 1536), BF16),
            pltpu.VMEM((3, 256, 1536), BF16),
            pltpu.VMEM((256, 1536), F32),
            pltpu.VMEM((128, 1536), BF16),
            pltpu.VMEM((128, 1536), BF16),
            pltpu.VMEM((2, 2, 128, 768), F32),
            pltpu.VMEM((2, 128, 768), F32),
            pltpu.VMEM((128, 1536), F32),
            pltpu.VMEM((4, 4, 2, SUB, 128), BF16),
            pltpu.VMEM((1536, 128), BF16),
            pltpu.VMEM((16, 48, 128), BF16),
            pltpu.VMEM((8, 16, 48, 256), BF16),
            pltpu.VMEM((2, 8, 128, 1536), BF16),
            pltpu.VMEM((8, 1, 1536), F32),
            pltpu.VMEM((4, SUB, 1024), BF16),
            pltpu.VMEM((768, 1536), F32),
            pltpu.VMEM((4, SUB, 384), BF16),
            pltpu.VMEM((2, 4, SUB, 384), F32),
            pltpu.VMEM((4, SUB, 384), F32),
            pltpu.VMEM((4, SUB, 384), BF16),
            pltpu.VMEM((2, 4, SUB, 384), F32),
            pltpu.VMEM((4, 8, 384), F32),
            pltpu.VMEM((3, 8, 384), F32),
            pltpu.VMEM((8, 72, 128), F32),
            pltpu.VMEM((7, 72, 128), F32),
            pltpu.VMEM((8, 72, 128), F32),
            pltpu.VMEM((7, 72, 128), F32),
            pltpu.VMEM((8, 32, 128), F32),
            pltpu.VMEM((7, 32, 128), F32),
            pltpu.VMEM((3, 3, 4, 48, 512), BF16),
            pltpu.VMEM((3, 3, 4, 48, 512), BF16),
            pltpu.VMEM((3, 4, 48, 512), BF16),
            pltpu.VMEM((3, 3, 48, 512), BF16),
            dma(8),
        ]
        + pairs((3,), (4,), (), (3, 2), (), (4,), (3,), (8,), (8,), (8,), ())
        + pairs((2,), (7,), (2,), (2,), (2,), (4, 2), (7,), (2,), (2, 2), (2, 2), (2, 2), (3, 3), (3,), (3, 7))
        + pairs((3, 3), (3, 3)),
        compiler_params=pltpu.CompilerParams(
            collective_id=0, has_side_effects=True, vmem_limit_bytes=62 * 2**20
        ),
    )(hidden, w_down.T, norm_gain.reshape(1, 192), w_up, grad_query.reshape(8, 128, 1536))
    return grad_down, grad_up, grad_gain.reshape(192)


def solution(mesh):
    placed = (P(("dp", "st"), None), P(None, "st"), P("st"), P(None, "st"), P("dp", "st"))
    return jax.shard_map(
        local,
        mesh=mesh,
        in_specs=placed,
        out_specs=(P("dp", "st"), P("dp", "st"), P("st")),
        check_vma=False,
    )
```

```python
import functools

import jax
import jax.numpy as jnp
from jax import lax
from jax.experimental import pallas as pl
from jax.experimental.pallas import tpu as pltpu
from jax.sharding import PartitionSpec as P

L = 1536
MESH = pl.DeviceIdType.MESH
F32 = jnp.float32
BF16 = jnp.bfloat16
SUB = 112
CUT = 80
PARTS = ((0, 48), (48, 48), (96, 16))


def coordinates():
    dp = lax.axis_index("dp")
    st = lax.axis_index("st")
    zl, y, c = dp // 8, lax.rem(dp // 2, 4), lax.rem(dp, 2)
    x, zh = st // 2, lax.rem(st, 2)
    return x, y, zh * 4 + zl, c


def device(x, y, z, c):
    x, y, z, c = lax.rem(x + 8, 4), lax.rem(y + 8, 4), lax.rem(z + 16, 8), lax.rem(c + 2, 2)
    return ((lax.rem(z, 4) * 4 + y) * 2 + c, x * 2 + z // 4)


def send(src, dst, send_sem, recv_sem, to):
    copy = pltpu.make_async_remote_copy(
        src_ref=src, dst_ref=dst, send_sem=send_sem, recv_sem=recv_sem, device_id=to, device_id_type=MESH
    )
    copy.start()
    return copy


def whole(
    hid, wdt, gain, wup_hbm, gq, gd_out, gu_out, gg_out,
    hidv, wdv, wup, gx, wt, hk, xb, gb, w, snd, rcv, own, zs, zr, lp, lx, nat, ht,
    nt, nts, ntx, gla, gpa, hr, g, xs, xf, xo, xr, xfr, xg, xgr, ea, ear, eb, ebr, ec, ecr, us, ur, vs, vr,
    loc_sem, x_s, x_r, g_s, g_r, h_s, h_r, n_s, n_r, q_s, q_r,
    za_s, za_r, zb_s, zb_r, yp_s, yp_r, ym_s, ym_r, yf_s, yf_r, l_s, l_r,
    c_s, c_r, t_s, t_r, glp_s, glp_r, glm_s, glm_r, glf_s, glf_r, glc_s, glc_r, gp_s, gp_r,
    z4_s, z4_r, np_s, np_r, nm_s, nm_r, nf_s, nf_r, d_s, d_r, dg_s, dg_r, e_s, e_r, u_s, u_r, v_s, v_r,
    wy_s, wy_r, wu_s, wu_r, wd_s, wd_r,
):
    x, y, z, c = coordinates()
    zh, zl = z // 4, lax.rem(z, 4)
    st = x * 2 + zh
    mine = y * 2 + c
    yc = [(dy, dc) for dy in (0, 1, 2, 3) for dc in (0, 1) if (dy, dc) != (0, 0)]
    s = 1 - 2 * c
    core_peer = device(x, y, z, c + 1)
    z4_peer = device(x, y, z + 4, c)
    up_x, down_x = device(x + 1, y, z, c), device(x - 1, y, z, c)
    up_y, down_y = device(x, y + 1, z, c), device(x, y - 1, z, c)
    far_y = device(x, y + 2, z, c)
    up_z, down_z = device(x, y, z + s, c), device(x, y, z - s, c)
    peers = (
        [device(x + d, y, z, c) for d in (1, 2, 3)] + [up_y, down_y, far_y, up_z, down_z, z4_peer, core_peer]
    )
    barrier = pltpu.get_barrier_semaphore()
    for peer in peers:
        pl.semaphore_signal(barrier, inc=1, device_id=peer, device_id_type=MESH)
    loads = [
        pltpu.make_async_copy(gq, gx.at[:, c], loc_sem.at[0]),
        pltpu.make_async_copy(wup_hbm, wup, loc_sem.at[1]),
        pltpu.make_async_copy(hid.at[:, pl.ds(pl.multiple_of(c * 1792, 128), 1792)], hk.at[c], loc_sem.at[2]),
        pltpu.make_async_copy(gain, gb.at[zh, x], loc_sem.at[3]),
        pltpu.make_async_copy(hid, hidv, loc_sem.at[6]),
    ]
    row = (c * 16 + y * 4 + zl) * SUB
    base = jnp.minimum(row // 128, 26) * 128
    window = pltpu.make_async_copy(wdt.at[:, pl.ds(pl.multiple_of(base, 128), 256)], wdv, loc_sem.at[7])
    window.start()
    loads[4].start()
    for load in loads[:4]:
        load.start()
    window.wait()
    wt[...] = wdv[...].astype(F32).T.astype(BF16)
    piece = wt.at[pl.ds(pl.multiple_of(row - base, 16), SUB)]
    my_piece = pltpu.make_async_copy(piece, xb.at[x], loc_sem.at[4])
    my_piece.start()
    sends = []

    def cotangent(owner, store):
        def tile(i, _):
            cols = pl.ds(pl.multiple_of(i * 256, 256), 256)
            store(
                cols,
                lax.dot_general(
                    gx[pl.ds(owner * 2, 2), c].reshape(256, 1536),
                    wup[cols, :],
                    (((1,), (1,)), ((), ())),
                    preferred_element_type=F32,
                ),
            )
            return 0

        lax.fori_loop(0, 6, tile, 0)

    far = pl.ds(pl.multiple_of((1 - zh) * 128, 128), 128)
    near = pl.ds(pl.multiple_of(zh * 128, 128), 128)
    n_copies = {}

    def partial_for(j, d):
        def store(cols, value):
            snd[j, :, cols] = value.astype(BF16)

        cotangent(lax.rem(x + d, 4), store)

    def keep(cols, value):
        own[:, cols] = value

    def send_partial(j, d, h, rows):
        n_copies[j, h] = send(
            snd.at[j, rows], rcv.at[j, rows], n_s.at[j, h], n_r.at[j, h], device(x + d, y, z, c)
        )

    def turn(i, _):
        cols = pl.ds(pl.multiple_of(i * 896, 128), 896)
        ht[i] = hidv[:, cols].astype(F32).T.astype(BF16).reshape(4, 2, SUB, 128)
        return 0

    loads[4].wait()
    lax.fori_loop(0, 4, turn, 0)
    loads[0].wait()
    loads[1].wait()
    partial_for(0, 2)
    partial_for(1, 1)
    pl.semaphore_wait(barrier, len(peers))

    x_copies = [
        send(piece, xb.at[x], x_s.at[d - 1], x_r.at[d - 1], device(x + d, y, z, c)) for d in (2, 1, 3)
    ]
    other_k = hid.at[:, pl.ds(pl.multiple_of((1 - c) * 1792, 128), 1792)]
    h_copy = send(other_k, hk.at[c], h_s, h_r, core_peer)
    g_copies = [
        send(gain, gb.at[zh, x], g_s.at[i], g_r.at[i], device(x + d, y, z, c)) for i, d in enumerate((2, 1, 3))
    ]
    gq_core = send(gq, gx.at[:, c], c_s.at[1], c_r.at[1], core_peer)
    sends += x_copies + [h_copy, gq_core] + g_copies

    partial_for(2, 3)
    my_piece.wait()
    for copy in x_copies:
        copy.wait_recv()
    loads[3].wait()
    for copy in g_copies:
        copy.wait_recv()
    g_across = send(gb.at[zh], gb.at[zh], g_s.at[3], g_r.at[3], z4_peer)
    sends += [g_across]

    def unit(zz, yy):
        zz, yy = lax.rem(zz + 16, 8), lax.rem(yy + 8, 4)
        return w.at[zz // 4, yy, lax.rem(zz, 4), pl.ds(0, CUT)]

    def slab(zz):
        zz = lax.rem(zz + 16, 8)
        return w.at[zz // 4, :, lax.rem(zz, 4), pl.ds(CUT, SUB - CUT)]

    for i in range(4):
        w[zh, y, zl, :, i * 192 : (i + 1) * 192] = xb[i]

    owners = [z, z - s, z + s, z - 2 * s, z + 2 * s, z - 3 * s, z + 3 * s, z - 4 * s]
    za, zb, yp, ym, yf = {}, {}, {}, {}, {}

    def pass_on(k):
        here = unit(owners[k], y)
        if k == 0 or (k % 2 == 1 and k < 7):
            i = (k + 1) // 2
            za[i] = send(here, here, za_s.at[i], za_r.at[i], up_z)
        if k == 0 or (k % 2 == 0 and k < 6):
            i = k // 2
            zb[i] = send(here, here, zb_s.at[i], zb_r.at[i], down_z)
        yp[k] = send(here, here, yp_s.at[k], yp_r.at[k], up_y)
        ym[k] = send(here, here, ym_s.at[k], ym_r.at[k], down_y)

    def forward(k):
        yp[k].wait_recv()
        ym[k].wait_recv()
        if k % 2 == 0:
            there = unit(owners[k], y - 1)
            yf[k] = send(there, there, yf_s.at[k], yf_r.at[k], up_y)
        else:
            there = unit(owners[k], y + 1)
            yf[k] = send(there, there, yf_s.at[k], yf_r.at[k], down_y)

    rest = w.at[zh, y, zl, pl.ds(CUT, SUB - CUT)]
    wy = [send(rest, rest, wy_s.at[i], wy_r.at[i], to) for i, to in enumerate((far_y, up_y, down_y))]
    wu, wd = {}, {}

    def climb(k):
        if k < 4:
            here = slab(z - s * k)
            wu[k] = send(here, here, wu_s.at[k], wu_r.at[k], up_z)
        if k < 3:
            here = slab(z + s * k)
            wd[k] = send(here, here, wd_s.at[k], wd_r.at[k], down_z)

    pass_on(0)
    for j, d in enumerate((2, 1, 3)):
        send_partial(j, d, 0, far)
    cotangent(x, keep)
    for copy in wy:
        copy.wait_recv()
    climb(0)
    za[0].wait_recv()
    pass_on(1)
    zb[0].wait_recv()
    pass_on(2)
    forward(0)
    wu[0].wait_recv()
    wd[0].wait_recv()
    climb(1)
    za[1].wait_recv()
    pass_on(3)
    zb[1].wait_recv()
    pass_on(4)
    forward(1)
    for j, d in enumerate((2, 1, 3)):
        n_copies[j, 0].wait_send()
        send_partial(j, d, 1, near)
    wu[1].wait_recv()
    wd[1].wait_recv()
    climb(2)
    za[2].wait_recv()
    pass_on(5)
    zb[2].wait_recv()
    pass_on(6)
    forward(2)
    wu[2].wait_recv()
    wd[2].wait_recv()
    climb(3)
    for j in range(3):
        n_copies[j, 0].wait_recv()
    total = own[far, :]
    for j in range(3):
        total = total + rcv[j, far, :].astype(F32)
    zs[...] = total.astype(BF16)
    q_copy = send(zs, zr, q_s, q_r, z4_peer)
    forward(3)
    za[3].wait_recv()
    pass_on(7)
    forward(4)
    forward(5)
    forward(6)
    forward(7)
    lanes_me = pl.ds(pl.multiple_of(mine * 128, 128), 128)
    t_copies = []
    for i, (dy, dc) in enumerate(yc):
        ty, tc = lax.rem(y + dy, 4), lax.rem(c + dc, 2)
        t_copies.append(
            send(ht.at[:, ty, tc], hr.at[:, :, lanes_me], t_s.at[i], t_r.at[i], device(x, y + dy, z, c + dc))
        )
    t_own = pltpu.make_async_copy(ht.at[:, y, c], hr.at[:, :, lanes_me], loc_sem.at[5])
    t_own.start()
    sends += t_copies
    for k in range(8):
        yf[k].wait_recv()
    wu[3].wait_recv()
    h_copy.wait_recv()
    loads[2].wait()

    l_copies = []
    for half in range(2):

        def tile(i, _):
            cols = pl.ds(pl.multiple_of(i * 256, 256), 256)
            value = jnp.dot(hk[...].reshape(256, 1792), w[half, :, :, :, cols].reshape(1792, 256), preferred_element_type=F32)
            lp[:, half, :, cols] = value.reshape(2, 128, 256)
            return 0

        lax.fori_loop(0, 3, tile, 0)
        l_copies.append(send(lp.at[1 - c, half], lx.at[half], l_s.at[half], l_r.at[half], core_peer))

    g_across.wait_recv()
    for j in range(3):
        n_copies[j, 1].wait_recv()
    q_copy.wait_recv()
    total = own[near, :] + zr[...].astype(F32)
    for j in range(3):
        total = total + rcv[j, near, :].astype(F32)
    own[0:128, :] = total
    for i in range(8):
        gpa[mine, :, i * 192 : (i + 1) * 192] = gb[i % 2, i // 2]
    for copy in l_copies:
        copy.wait_recv()
    for half in range(2):
        for i in range(4):
            piece_cols = pl.ds(i * 192, 192)
            at = i * 384 + half * 192
            nat[:, at : at + 192] = lp[c, half, :, piece_cols] + lx[half, :, piece_cols]
    latent = nat[...]
    inverse = lax.rsqrt(jnp.sum(latent * latent, axis=1, keepdims=True) / L + 1e-06)
    for i in range(12):
        cols = pl.ds(i * 128, 128)
        nt[cols, :] = (nat[:, cols] * inverse * gpa[mine, :, cols]).T.astype(BF16)
    lanes_c = pl.ds(pl.multiple_of(c * 128, 128), 128)
    for i in range(16):
        nts[i] = nt[pl.ds(pl.multiple_of(i * 96 + (1 - c) * 48, 16), 48), :]
    nt_core = send(nts, ntx.at[st, :, :, lanes_c], c_s.at[0], c_r.at[0], core_peer)
    for i in range(16):
        ntx[st, i, :, lanes_c] = nt[pl.ds(pl.multiple_of(i * 96 + c * 48, 16), 48), :]
    inner = jnp.sum(gpa[mine] * own[0:128, :] * nat[...], axis=1, keepdims=True)
    factor = inverse**3 * inner / L
    for i in range(12):
        cols = pl.ds(i * 128, 128)
        lat, cot = nat[:, cols], own[0:128, cols]
        value = inverse * gpa[mine, :, cols] * cot - lat * factor
        high = value.astype(BF16)
        gla[0, mine, :, cols] = high
        gla[1, mine, :, cols] = (value - high.astype(F32)).astype(BF16)
        gpa[mine, :, cols] = jnp.sum(cot * lat * inverse, axis=0, keepdims=True)

    mine_gl = [gla.at[v, mine] for v in range(2)]
    glp = [send(mine_gl[0], mine_gl[0], glp_s.at[0], glp_r.at[0], up_y)]
    glm = [send(mine_gl[0], mine_gl[0], glm_s.at[0], glm_r.at[0], down_y)]

    def part(slot, h):
        return ntx.at[slot, pl.ds(h * 8, 8)]

    nt_core.wait_recv()
    z4 = [send(part(st, h), part(st, h), z4_s.at[h], z4_r.at[h], z4_peer) for h in range(2)]
    np_, nm, nf = {}, {}, {}

    def spread(a, slot, order):
        for up, h in order:
            there = part(slot, h)
            if up:
                np_[a, h] = send(there, there, np_s.at[a, h], np_r.at[a, h], up_x)
            else:
                nm[a, h] = send(there, there, nm_s.at[a, h], nm_r.at[a, h], down_x)

    def relay(a, side):
        np_[a, 0].wait_recv()
        there = part(lax.rem(x + 3, 4) * 2 + side, 0)
        nf[a, 0] = send(there, there, nf_s.at[a, 0], nf_r.at[a, 0], up_x)
        nm[a, 1].wait_recv()
        there = part(lax.rem(x + 1, 4) * 2 + side, 1)
        nf[a, 1] = send(there, there, nf_s.at[a, 1], nf_r.at[a, 1], down_x)

    spread(0, st, ((True, 0), (False, 1), (False, 0), (True, 1)))
    glp.append(send(mine_gl[1], mine_gl[1], glp_s.at[1], glp_r.at[1], up_y))
    glm.append(send(mine_gl[1], mine_gl[1], glm_s.at[1], glm_r.at[1], down_y))
    gp_copies = [
        send(gpa.at[mine], gpa.at[mine], gp_s.at[i], gp_r.at[i], device(x, y + dy, z, c + dc))
        for i, (dy, dc) in enumerate(yc)
    ]
    glc = [send(mine_gl[v], mine_gl[v], glc_s.at[0, v], glc_r.at[0, v], core_peer) for v in range(2)]
    relay(0, zh)

    def to_core(v, i, dy):
        slot = gla.at[v, lax.rem(y + dy, 4) * 2 + c]
        glc.append(send(slot, slot, glc_s.at[i, v], glc_r.at[i, v], core_peer))
        return slot

    glp[0].wait_recv()
    slot = to_core(0, 1, 3)
    glf = [send(slot, slot, glf_s.at[0], glf_r.at[0], up_y)]
    glm[0].wait_recv()
    to_core(0, 2, 1)
    side = 1 - zh
    other = x * 2 + side
    z4[0].wait_recv()
    spread(1, other, ((True, 0), (False, 0)))

    def product(zz, cols):
        value = None
        for i in range(4):
            slot = i * 2 + zz
            term = jnp.dot(
                ntx[slot].reshape(768, 256), gx[slot, :, :, cols].reshape(256, 256), preferred_element_type=F32
            )
            value = term if value is None else value + term
        return value

    gq_core.wait_recv()
    np_[0, 1].wait_recv()
    nm[0, 0].wait_recv()
    nf[0, 0].wait_recv()
    nf[0, 1].wait_recv()

    def first(i, _):
        cols = pl.ds(pl.multiple_of(i * 256, 256), 256)
        g[:, cols] = product(zh, cols)
        return 0

    lax.fori_loop(0, 3, first, 0)
    z4[1].wait_recv()
    spread(1, other, ((False, 1), (True, 1)))
    glm[1].wait_recv()
    slot = to_core(1, 2, 1)
    glf.append(send(slot, slot, glf_s.at[1], glf_r.at[1], down_y))
    glp[1].wait_recv()
    to_core(1, 1, 3)
    lax.fori_loop(3, 6, first, 0)
    relay(1, side)
    glf[0].wait_recv()
    to_core(0, 3, 2)
    glf[1].wait_recv()
    to_core(1, 3, 2)
    sends += z4 + glp + glm + glf + glc + gp_copies + [nt_core]

    t_own.wait()
    for copy in glc + gp_copies + t_copies:
        copy.wait_recv()
    d_copies, dg_copies = {}, []
    split = [pl.ds(begin, size) for begin, size in PARTS]

    def outgoing(j):
        return xs if j == 0 else xf.at[j - 1]

    def arrived(j):
        return xr if j == 0 else xfr.at[j - 1]

    def send_down(j, d, h):
        d_copies[j, h] = send(
            outgoing(j).at[:, split[h]], arrived(j).at[:, split[h]],
            d_s.at[j, h], d_r.at[j, h], device(x + d, y, z, c),
        )

    for j, d in enumerate((2, 1, 3, 0)):
        to = lax.rem(x + d, 4)
        cols = pl.ds(pl.multiple_of(to * 384, 128), 384)
        rows = hr[...].reshape(448, 1024)
        value = jnp.dot(rows, gla[0, :, :, cols].reshape(1024, 384), preferred_element_type=F32) + jnp.dot(
            rows, gla[1, :, :, cols].reshape(1024, 384), preferred_element_type=F32
        )
        value = value.reshape(4, SUB, 384)
        total = gpa[0, :, cols]
        for i in range(1, 8):
            total = total + gpa[i, :, cols]
        xg[j] = jnp.broadcast_to(total, (8, 384))
        if d:
            outgoing(j)[...] = value.astype(outgoing(j).dtype)
            send_down(j, d, 0)
            dg_copies.append(send(xg.at[j], xgr.at[j], dg_s.at[j], dg_r.at[j], device(x + d, y, z, c)))
        else:
            xo[...] = value
    for h in (1, 2):
        for j, d in enumerate((2, 1, 3)):
            send_down(j, d, h)
    sends += list(d_copies.values()) + dg_copies

    np_[1, 1].wait_recv()
    nm[1, 0].wait_recv()
    nf[1, 0].wait_recv()
    nf[1, 1].wait_recv()
    sends += list(np_.values()) + list(nm.values()) + list(nf.values())
    u_copies = {}
    for n in range(3):

        def second(i, _):
            cols = pl.ds(pl.multiple_of(n * 512 + i * 256, 256), 256)
            g[:, cols] = g[:, cols] + product(1 - zh, cols)
            return 0

        lax.fori_loop(0, 2, second, 0)
        cols = pl.ds(n * 512, 512)
        for j, d in enumerate((2, 1, 3)):
            ty = lax.rem(y + d, 4)
            for k in range(4):
                rows = pl.ds(pl.multiple_of((k * 4 + ty) * 48, 16), 48)
                us[n, j, k] = g[rows, cols].astype(BF16)
            u_copies[n, j] = send(us.at[n, j], ur.at[n, j], u_s.at[n, j], u_r.at[n, j], device(x, y + d, z, c))
    sends += list(u_copies.values())

    v_copies = {}

    def narrow(n):
        cols = pl.ds(n * 512, 512)
        for j in range(3):
            u_copies[n, j].wait_recv()
        for k in range(4):
            rows = pl.ds(pl.multiple_of((k * 4 + y) * 48, 16), 48)
            total = g[rows, cols]
            for j in range(3):
                total = total + ur[n, j, k].astype(F32)
            g[rows, cols] = total
            vs[n, k] = total.astype(BF16)
        for d in (2, 1, 3):
            to = lax.rem(zl + d, 4)
            v_copies[n, d] = send(
                vs.at[n, to], vr.at[n, d - 1], v_s.at[n, d - 1], v_r.at[n, d - 1], device(x, y, zh * 4 + to, c)
            )

    e_copies = {}

    def deliver(h, buffer, landing):
        begin, size = PARTS[h]
        for j in range(3):
            d_copies[j, h].wait_recv()
        for b in range(4):
            total = xo[b, begin : begin + size, :]
            for j in range(3):
                total = total + arrived(j)[b, begin : begin + size, :].astype(F32)
            xo[b, begin : begin + size, :] = total
            for a in range(2):
                at, mid = a * 192, begin + size // 2
                i = a * 4 + b
                buffer[i, 0:size, :] = xo[b, begin : begin + size, at : at + 128]
                buffer[i, size : size + size // 2, 0:64] = xo[b, begin:mid, at + 128 : at + 192]
                buffer[i, size : size + size // 2, 64:128] = xo[b, mid : begin + size, at + 128 : at + 192]
        if h == 2:
            for copy in dg_copies:
                copy.wait_recv()
            total = xg[3]
            for j in range(3):
                total = total + xgr[j]
            xg[3] = total
            for a in range(2):
                for b in range(4):
                    buffer[a * 4 + b, 24:32, :] = jnp.zeros((8, 128), F32)
                    buffer[a * 4 + b, 24:25, :] = xg[3, 0:1, a * 192 : a * 192 + 128]
                    buffer[a * 4 + b, 25:26, 0:64] = xg[3, 0:1, a * 192 + 128 : a * 192 + 192]
        for d in (4, 3, 5, 2, 6, 1, 7):
            e_copies[h, d] = send(
                buffer.at[lax.rem(z + d, 8)], landing.at[d - 1],
                e_s.at[h, d - 1], e_r.at[h, d - 1], device(x, y, z + d, c),
            )

    deliver(0, ea, ear)
    narrow(0)
    narrow(1)
    deliver(1, eb, ebr)
    deliver(2, ec, ecr)
    narrow(2)
    sends += list(v_copies.values()) + list(e_copies.values())

    for h, (buffer, landing) in enumerate(((ea, ear), (eb, ebr), (ec, ecr))):
        begin, size = PARTS[h]
        for d in range(1, 8):
            e_copies[h, d].wait_recv()
        total = buffer[z]
        for j in range(7):
            total = total + landing[j]
        half = size // 2
        gd_out[begin : begin + size, 0:128] = total[0:size]
        gd_out[begin : begin + half, 128:192] = total[size : size + half, 0:64]
        gd_out[begin + half : begin + size, 128:192] = total[size : size + half, 64:128]
        if h == 2:
            gg_out[:, 0:128] = total[24:25]
            gg_out[:, 128:192] = total[25:26, 0:64]
    my_rows = pl.ds(pl.multiple_of((zl * 4 + y) * 48, 16), 48)
    for n in range(3):
        cols = pl.ds(n * 512, 512)
        for d in (1, 2, 3):
            v_copies[n, d].wait_recv()
        total = g[my_rows, cols]
        for j in range(3):
            total = total + vr[n, j].astype(F32)
        gu_out[:, cols] = total
    sends += [n_copies[j, 1] for j in range(3)] + [q_copy] + l_copies + wy
    for group in (za, zb, yp, ym, yf, wu, wd):
        sends += list(group.values())
    for copy in sends:
        copy.wait_send()


VMEM = pl.BlockSpec(memory_space=pltpu.VMEM)
ANY = pl.BlockSpec(memory_space=pl.ANY)


def dma(*shape):
    return pltpu.SemaphoreType.DMA(shape) if shape else pltpu.SemaphoreType.DMA


def pairs(*shapes):
    return [dma(*shape) for shape in shapes for _ in range(2)]


def local(hidden, w_down, norm_gain, w_up, grad_query):
    grad_down, grad_up, grad_gain = pl.pallas_call(
        whole,
        out_shape=(
            jax.ShapeDtypeStruct((112, 192), F32),
            jax.ShapeDtypeStruct((48, 1536), F32),
            jax.ShapeDtypeStruct((1, 192), F32),
        ),
        in_specs=[ANY, ANY, VMEM, ANY, ANY],
        out_specs=(VMEM, VMEM, VMEM),
        scratch_shapes=[
            pltpu.VMEM((128, 3584), BF16),
            pltpu.VMEM((192, 256), BF16),
            pltpu.VMEM((1536, 1536), BF16),
            pltpu.VMEM((8, 2, 128, 1536), BF16),
            pltpu.VMEM((256, 192), BF16),
            pltpu.VMEM((2, 128, 1792), BF16),
            pltpu.VMEM((4, SUB, 192), BF16),
            pltpu.VMEM((2, 4, 1, 192), F32),
            pltpu.VMEM((2, 4, 4, SUB, 768), BF16),
            pltpu.VMEM((3, 256, 1536), BF16),
            pltpu.VMEM((3, 256, 1536), BF16),
            pltpu.VMEM((256, 1536), F32),
            pltpu.VMEM((128, 1536), BF16),
            pltpu.VMEM((128, 1536), BF16),
            pltpu.VMEM((2, 2, 128, 768), F32),
            pltpu.VMEM((2, 128, 768), F32),
            pltpu.VMEM((128, 1536), F32),
            pltpu.VMEM((4, 4, 2, SUB, 128), BF16),
            pltpu.VMEM((1536, 128), BF16),
            pltpu.VMEM((16, 48, 128), BF16),
            pltpu.VMEM((8, 16, 48, 256), BF16),
            pltpu.VMEM((2, 8, 128, 1536), BF16),
            pltpu.VMEM((8, 1, 1536), F32),
            pltpu.VMEM((4, SUB, 1024), BF16),
            pltpu.VMEM((768, 1536), F32),
            pltpu.VMEM((4, SUB, 384), BF16),
            pltpu.VMEM((2, 4, SUB, 384), F32),
            pltpu.VMEM((4, SUB, 384), F32),
            pltpu.VMEM((4, SUB, 384), BF16),
            pltpu.VMEM((2, 4, SUB, 384), F32),
            pltpu.VMEM((4, 8, 384), F32),
            pltpu.VMEM((3, 8, 384), F32),
            pltpu.VMEM((8, 72, 128), F32),
            pltpu.VMEM((7, 72, 128), F32),
            pltpu.VMEM((8, 72, 128), F32),
            pltpu.VMEM((7, 72, 128), F32),
            pltpu.VMEM((8, 32, 128), F32),
            pltpu.VMEM((7, 32, 128), F32),
            pltpu.VMEM((3, 3, 4, 48, 512), BF16),
            pltpu.VMEM((3, 3, 4, 48, 512), BF16),
            pltpu.VMEM((3, 4, 48, 512), BF16),
            pltpu.VMEM((3, 3, 48, 512), BF16),
            dma(8),
        ]
        + pairs((3,), (4,), (), (3, 2), (), (4,), (3,), (8,), (8,), (8,), (2,))
        + pairs((2,), (7,), (2,), (2,), (2,), (4, 2), (7,), (2,), (2, 2), (2, 2), (2, 2), (3, 3), (3,), (3, 7))
        + pairs((3, 3), (3, 3), (3,), (4,), (3,)),
        compiler_params=pltpu.CompilerParams(
            collective_id=0, has_side_effects=True, vmem_limit_bytes=62 * 2**20
        ),
    )(hidden, w_down.T, norm_gain.reshape(1, 192), w_up, grad_query.reshape(8, 128, 1536))
    return grad_down, grad_up, grad_gain.reshape(192)


def solution(mesh):
    placed = (P(("dp", "st"), None), P(None, "st"), P("st"), P(None, "st"), P("dp", "st"))
    return jax.shard_map(
        local,
        mesh=mesh,
        in_specs=placed,
        out_specs=(P("dp", "st"), P("dp", "st"), P("st")),
        check_vma=False,
    )
```

```python
import functools

import jax
import jax.numpy as jnp
from jax import lax
from jax.experimental import pallas as pl
from jax.experimental.pallas import tpu as pltpu
from jax.sharding import PartitionSpec as P

L = 1536
MESH = pl.DeviceIdType.MESH
F32 = jnp.float32
BF16 = jnp.bfloat16
SUB = 112
CUT = 80
PARTS = ((0, 48), (48, 48), (96, 16))


def coordinates():
    dp = lax.axis_index("dp")
    st = lax.axis_index("st")
    zl, y, c = dp // 8, lax.rem(dp // 2, 4), lax.rem(dp, 2)
    x, zh = st // 2, lax.rem(st, 2)
    return x, y, zh * 4 + zl, c


def device(x, y, z, c):
    x, y, z, c = lax.rem(x + 8, 4), lax.rem(y + 8, 4), lax.rem(z + 16, 8), lax.rem(c + 2, 2)
    return ((lax.rem(z, 4) * 4 + y) * 2 + c, x * 2 + z // 4)


def send(src, dst, send_sem, recv_sem, to):
    copy = pltpu.make_async_remote_copy(
        src_ref=src, dst_ref=dst, send_sem=send_sem, recv_sem=recv_sem, device_id=to, device_id_type=MESH
    )
    copy.start()
    return copy


def whole(
    hid, wdt, gain, wup_hbm, gq, gd_out, gu_out, gg_out,
    hidv, wdv, wup, gx, wt, hk, xb, gb, w, snd, rcv, own, zs, zr, lp, lx, nat, ht,
    nt, nts, ntx, gla, gpa, hr, g, xs, xf, xo, xr, xfr, xg, xgr, ea, ear, eb, ebr, ec, ecr, us, ur, vs, vr,
    loc_sem, x_s, x_r, g_s, g_r, h_s, h_r, n_s, n_r, q_s, q_r,
    za_s, za_r, zb_s, zb_r, yp_s, yp_r, ym_s, ym_r, yf_s, yf_r, l_s, l_r,
    c_s, c_r, t_s, t_r, glp_s, glp_r, glm_s, glm_r, glf_s, glf_r, glc_s, glc_r, gp_s, gp_r,
    z4_s, z4_r, np_s, np_r, nm_s, nm_r, nf_s, nf_r, d_s, d_r, dg_s, dg_r, e_s, e_r, u_s, u_r, v_s, v_r,
    wy_s, wy_r, wu_s, wu_r, wd_s, wd_r,
):
    x, y, z, c = coordinates()
    zh, zl = z // 4, lax.rem(z, 4)
    st = x * 2 + zh
    mine = y * 2 + c
    yc = [(dy, dc) for dy in (0, 1, 2, 3) for dc in (0, 1) if (dy, dc) != (0, 0)]
    s = 1 - 2 * c
    core_peer = device(x, y, z, c + 1)
    z4_peer = device(x, y, z + 4, c)
    up_x, down_x = device(x + 1, y, z, c), device(x - 1, y, z, c)
    up_y, down_y = device(x, y + 1, z, c), device(x, y - 1, z, c)
    far_y = device(x, y + 2, z, c)
    up_z, down_z = device(x, y, z + s, c), device(x, y, z - s, c)
    peers = (
        [device(x + d, y, z, c) for d in (1, 2, 3)] + [up_y, down_y, far_y, up_z, down_z, z4_peer, core_peer]
    )
    barrier = pltpu.get_barrier_semaphore()
    for peer in peers:
        pl.semaphore_signal(barrier, inc=1, device_id=peer, device_id_type=MESH)
    loads = [
        pltpu.make_async_copy(gq, gx.at[:, c], loc_sem.at[0]),
        pltpu.make_async_copy(wup_hbm, wup, loc_sem.at[1]),
        pltpu.make_async_copy(hid.at[:, pl.ds(pl.multiple_of(c * 1792, 128), 1792)], hk.at[c], loc_sem.at[2]),
        pltpu.make_async_copy(gain, gb.at[zh, x], loc_sem.at[3]),
        pltpu.make_async_copy(hid, hidv, loc_sem.at[6]),
    ]
    row = (c * 16 + y * 4 + zl) * SUB
    base = jnp.minimum(row // 128, 26) * 128
    window = pltpu.make_async_copy(wdt.at[:, pl.ds(pl.multiple_of(base, 128), 256)], wdv, loc_sem.at[7])
    window.start()
    loads[4].start()
    for load in loads[:4]:
        load.start()
    window.wait()
    wt[...] = wdv[...].astype(F32).T.astype(BF16)
    piece = wt.at[pl.ds(pl.multiple_of(row - base, 16), SUB)]
    my_piece = pltpu.make_async_copy(piece, xb.at[x], loc_sem.at[4])
    my_piece.start()
    sends = []

    def cotangent(owner, store):
        def tile(i, _):
            cols = pl.ds(pl.multiple_of(i * 256, 256), 256)
            store(
                cols,
                lax.dot_general(
                    gx[pl.ds(owner * 2, 2), c].reshape(256, 1536),
                    wup[cols, :],
                    (((1,), (1,)), ((), ())),
                    preferred_element_type=F32,
                ),
            )
            return 0

        lax.fori_loop(0, 6, tile, 0)

    far = pl.ds(pl.multiple_of((1 - zh) * 128, 128), 128)
    near = pl.ds(pl.multiple_of(zh * 128, 128), 128)
    n_copies = {}

    def partial_for(j, d):
        def store(cols, value):
            snd[j, :, cols] = value.astype(BF16)

        cotangent(lax.rem(x + d, 4), store)

    def keep(cols, value):
        own[:, cols] = value

    def send_partial(j, d, h, rows):
        n_copies[j, h] = send(
            snd.at[j, rows], rcv.at[j, rows], n_s.at[j, h], n_r.at[j, h], device(x + d, y, z, c)
        )

    def turn(i, _):
        cols = pl.ds(pl.multiple_of(i * 896, 128), 896)
        ht[i] = hidv[:, cols].astype(F32).T.astype(BF16).reshape(4, 2, SUB, 128)
        return 0

    loads[4].wait()
    lax.fori_loop(0, 4, turn, 0)
    loads[0].wait()
    loads[1].wait()
    partial_for(0, 2)
    partial_for(1, 1)
    pl.semaphore_wait(barrier, len(peers))

    x_copies = [
        send(piece, xb.at[x], x_s.at[d - 1], x_r.at[d - 1], device(x + d, y, z, c)) for d in (2, 1, 3)
    ]
    other_k = hid.at[:, pl.ds(pl.multiple_of((1 - c) * 1792, 128), 1792)]
    h_copy = send(other_k, hk.at[c], h_s, h_r, core_peer)
    g_copies = [
        send(gain, gb.at[zh, x], g_s.at[i], g_r.at[i], device(x + d, y, z, c)) for i, d in enumerate((2, 1, 3))
    ]
    gq_core = send(gq, gx.at[:, c], c_s.at[1], c_r.at[1], core_peer)
    sends += x_copies + [h_copy, gq_core] + g_copies

    partial_for(2, 3)
    my_piece.wait()
    for copy in x_copies:
        copy.wait_recv()
    loads[3].wait()
    for copy in g_copies:
        copy.wait_recv()
    g_across = send(gb.at[zh], gb.at[zh], g_s.at[3], g_r.at[3], z4_peer)
    sends += [g_across]

    def unit(zz, yy):
        zz, yy = lax.rem(zz + 16, 8), lax.rem(yy + 8, 4)
        return w.at[zz // 4, yy, lax.rem(zz, 4), pl.ds(0, CUT)]

    def slab(zz):
        zz = lax.rem(zz + 16, 8)
        return w.at[zz // 4, :, lax.rem(zz, 4), pl.ds(CUT, SUB - CUT)]

    for i in range(4):
        w[zh, y, zl, :, i * 192 : (i + 1) * 192] = xb[i]

    owners = [z, z - s, z + s, z - 2 * s, z + 2 * s, z - 3 * s, z + 3 * s, z - 4 * s]
    za, zb, yp, ym, yf = {}, {}, {}, {}, {}

    def pass_on(k):
        here = unit(owners[k], y)
        if k == 0 or (k % 2 == 1 and k < 7):
            i = (k + 1) // 2
            za[i] = send(here, here, za_s.at[i], za_r.at[i], up_z)
        if k == 0 or (k % 2 == 0 and k < 6):
            i = k // 2
            zb[i] = send(here, here, zb_s.at[i], zb_r.at[i], down_z)
        if k == 7:
            yf[k] = send(here, here, yf_s.at[k], yf_r.at[k], far_y)
        yp[k] = send(here, here, yp_s.at[k], yp_r.at[k], up_y)
        ym[k] = send(here, here, ym_s.at[k], ym_r.at[k], down_y)

    def forward(k):
        yp[k].wait_recv()
        ym[k].wait_recv()
        if k == 7:
            return
        if k % 2 == 0:
            there = unit(owners[k], y - 1)
            yf[k] = send(there, there, yf_s.at[k], yf_r.at[k], up_y)
        else:
            there = unit(owners[k], y + 1)
            yf[k] = send(there, there, yf_s.at[k], yf_r.at[k], down_y)

    rest = w.at[zh, y, zl, pl.ds(CUT, SUB - CUT)]
    wy = [send(rest, rest, wy_s.at[i], wy_r.at[i], to) for i, to in enumerate((far_y, up_y, down_y))]
    wu, wd = {}, {}

    def climb(k):
        if k < 4:
            here = slab(z - s * k)
            wu[k] = send(here, here, wu_s.at[k], wu_r.at[k], up_z)
        if k < 3:
            here = slab(z + s * k)
            wd[k] = send(here, here, wd_s.at[k], wd_r.at[k], down_z)

    pass_on(0)
    for j, d in enumerate((2, 1, 3)):
        send_partial(j, d, 0, far)
    cotangent(x, keep)
    for copy in wy:
        copy.wait_recv()
    climb(0)
    za[0].wait_recv()
    pass_on(1)
    zb[0].wait_recv()
    pass_on(2)
    forward(0)
    wu[0].wait_recv()
    wd[0].wait_recv()
    climb(1)
    za[1].wait_recv()
    pass_on(3)
    zb[1].wait_recv()
    pass_on(4)
    forward(1)
    for j, d in enumerate((2, 1, 3)):
        n_copies[j, 0].wait_send()
        send_partial(j, d, 1, near)
    wu[1].wait_recv()
    wd[1].wait_recv()
    climb(2)
    za[2].wait_recv()
    pass_on(5)
    zb[2].wait_recv()
    pass_on(6)
    forward(2)
    wu[2].wait_recv()
    wd[2].wait_recv()
    climb(3)
    for j in range(3):
        n_copies[j, 0].wait_recv()
    total = own[far, :]
    for j in range(3):
        total = total + rcv[j, far, :].astype(F32)
    zs[...] = total.astype(BF16)
    q_copy = send(zs, zr, q_s, q_r, z4_peer)
    forward(3)
    za[3].wait_recv()
    pass_on(7)
    forward(4)
    forward(5)
    forward(6)
    forward(7)
    lanes_me = pl.ds(pl.multiple_of(mine * 128, 128), 128)
    t_copies = []
    for i, (dy, dc) in enumerate(yc):
        ty, tc = lax.rem(y + dy, 4), lax.rem(c + dc, 2)
        t_copies.append(
            send(ht.at[:, ty, tc], hr.at[:, :, lanes_me], t_s.at[i], t_r.at[i], device(x, y + dy, z, c + dc))
        )
    t_own = pltpu.make_async_copy(ht.at[:, y, c], hr.at[:, :, lanes_me], loc_sem.at[5])
    t_own.start()
    sends += t_copies
    for k in range(8):
        yf[k].wait_recv()
    wu[3].wait_recv()
    h_copy.wait_recv()
    loads[2].wait()

    l_copies = []
    for half in range(2):

        def tile(i, _):
            cols = pl.ds(pl.multiple_of(i * 256, 256), 256)
            value = jnp.dot(hk[...].reshape(256, 1792), w[half, :, :, :, cols].reshape(1792, 256), preferred_element_type=F32)
            lp[:, half, :, cols] = value.reshape(2, 128, 256)
            return 0

        lax.fori_loop(0, 3, tile, 0)
        l_copies.append(send(lp.at[1 - c, half], lx.at[half], l_s.at[half], l_r.at[half], core_peer))

    g_across.wait_recv()
    for j in range(3):
        n_copies[j, 1].wait_recv()
    q_copy.wait_recv()
    total = own[near, :] + zr[...].astype(F32)
    for j in range(3):
        total = total + rcv[j, near, :].astype(F32)
    own[0:128, :] = total
    for i in range(8):
        gpa[mine, :, i * 192 : (i + 1) * 192] = gb[i % 2, i // 2]
    for copy in l_copies:
        copy.wait_recv()
    for half in range(2):
        for i in range(4):
            piece_cols = pl.ds(i * 192, 192)
            at = i * 384 + half * 192
            nat[:, at : at + 192] = lp[c, half, :, piece_cols] + lx[half, :, piece_cols]
    latent = nat[...]
    inverse = lax.rsqrt(jnp.sum(latent * latent, axis=1, keepdims=True) / L + 1e-06)
    for i in range(12):
        cols = pl.ds(i * 128, 128)
        nt[cols, :] = (nat[:, cols] * inverse * gpa[mine, :, cols]).T.astype(BF16)
    lanes_c = pl.ds(pl.multiple_of(c * 128, 128), 128)
    for i in range(16):
        nts[i] = nt[pl.ds(pl.multiple_of(i * 96 + (1 - c) * 48, 16), 48), :]
    nt_core = send(nts, ntx.at[st, :, :, lanes_c], c_s.at[0], c_r.at[0], core_peer)
    for i in range(16):
        ntx[st, i, :, lanes_c] = nt[pl.ds(pl.multiple_of(i * 96 + c * 48, 16), 48), :]
    inner = jnp.sum(gpa[mine] * own[0:128, :] * nat[...], axis=1, keepdims=True)
    factor = inverse**3 * inner / L
    for i in range(12):
        cols = pl.ds(i * 128, 128)
        lat, cot = nat[:, cols], own[0:128, cols]
        value = inverse * gpa[mine, :, cols] * cot - lat * factor
        high = value.astype(BF16)
        gla[0, mine, :, cols] = high
        gla[1, mine, :, cols] = (value - high.astype(F32)).astype(BF16)
        gpa[mine, :, cols] = jnp.sum(cot * lat * inverse, axis=0, keepdims=True)

    mine_gl = [gla.at[v, mine] for v in range(2)]
    glp = [send(mine_gl[0], mine_gl[0], glp_s.at[0], glp_r.at[0], up_y)]
    glm = [send(mine_gl[0], mine_gl[0], glm_s.at[0], glm_r.at[0], down_y)]

    def part(slot, h):
        return ntx.at[slot, pl.ds(h * 8, 8)]

    nt_core.wait_recv()
    z4 = [send(part(st, h), part(st, h), z4_s.at[h], z4_r.at[h], z4_peer) for h in range(2)]
    np_, nm, nf = {}, {}, {}

    def spread(a, slot, order):
        for up, h in order:
            there = part(slot, h)
            if up:
                np_[a, h] = send(there, there, np_s.at[a, h], np_r.at[a, h], up_x)
            else:
                nm[a, h] = send(there, there, nm_s.at[a, h], nm_r.at[a, h], down_x)

    def relay(a, side):
        np_[a, 0].wait_recv()
        there = part(lax.rem(x + 3, 4) * 2 + side, 0)
        nf[a, 0] = send(there, there, nf_s.at[a, 0], nf_r.at[a, 0], up_x)
        nm[a, 1].wait_recv()
        there = part(lax.rem(x + 1, 4) * 2 + side, 1)
        nf[a, 1] = send(there, there, nf_s.at[a, 1], nf_r.at[a, 1], down_x)

    spread(0, st, ((True, 0), (False, 1), (False, 0), (True, 1)))
    glp.append(send(mine_gl[1], mine_gl[1], glp_s.at[1], glp_r.at[1], up_y))
    glm.append(send(mine_gl[1], mine_gl[1], glm_s.at[1], glm_r.at[1], down_y))
    gp_copies = [
        send(gpa.at[mine], gpa.at[mine], gp_s.at[i], gp_r.at[i], device(x, y + dy, z, c + dc))
        for i, (dy, dc) in enumerate(yc)
    ]
    glc = [send(mine_gl[v], mine_gl[v], glc_s.at[0, v], glc_r.at[0, v], core_peer) for v in range(2)]
    relay(0, zh)

    def to_core(v, i, dy):
        slot = gla.at[v, lax.rem(y + dy, 4) * 2 + c]
        glc.append(send(slot, slot, glc_s.at[i, v], glc_r.at[i, v], core_peer))
        return slot

    glp[0].wait_recv()
    slot = to_core(0, 1, 3)
    glf = [send(slot, slot, glf_s.at[0], glf_r.at[0], up_y)]
    glm[0].wait_recv()
    to_core(0, 2, 1)
    side = 1 - zh
    other = x * 2 + side
    z4[0].wait_recv()
    spread(1, other, ((True, 0), (False, 0)))

    def product(zz, cols):
        value = None
        for i in range(4):
            slot = i * 2 + zz
            term = jnp.dot(
                ntx[slot].reshape(768, 256), gx[slot, :, :, cols].reshape(256, 256), preferred_element_type=F32
            )
            value = term if value is None else value + term
        return value

    gq_core.wait_recv()
    np_[0, 1].wait_recv()
    nm[0, 0].wait_recv()
    nf[0, 0].wait_recv()
    nf[0, 1].wait_recv()

    def first(i, _):
        cols = pl.ds(pl.multiple_of(i * 256, 256), 256)
        g[:, cols] = product(zh, cols)
        return 0

    lax.fori_loop(0, 3, first, 0)
    z4[1].wait_recv()
    spread(1, other, ((False, 1), (True, 1)))
    glm[1].wait_recv()
    slot = to_core(1, 2, 1)
    glf.append(send(slot, slot, glf_s.at[1], glf_r.at[1], down_y))
    glp[1].wait_recv()
    to_core(1, 1, 3)
    lax.fori_loop(3, 6, first, 0)
    relay(1, side)
    glf[0].wait_recv()
    to_core(0, 3, 2)
    glf[1].wait_recv()
    to_core(1, 3, 2)
    sends += z4 + glp + glm + glf + glc + gp_copies + [nt_core]

    t_own.wait()
    for copy in glc + gp_copies + t_copies:
        copy.wait_recv()
    d_copies, dg_copies = {}, []
    split = [pl.ds(begin, size) for begin, size in PARTS]

    def outgoing(j):
        return xs if j == 0 else xf.at[j - 1]

    def arrived(j):
        return xr if j == 0 else xfr.at[j - 1]

    def send_down(j, d, h):
        d_copies[j, h] = send(
            outgoing(j).at[:, split[h]], arrived(j).at[:, split[h]],
            d_s.at[j, h], d_r.at[j, h], device(x + d, y, z, c),
        )

    for j, d in enumerate((2, 1, 3, 0)):
        to = lax.rem(x + d, 4)
        cols = pl.ds(pl.multiple_of(to * 384, 128), 384)
        rows = hr[...].reshape(448, 1024)
        value = jnp.dot(rows, gla[0, :, :, cols].reshape(1024, 384), preferred_element_type=F32) + jnp.dot(
            rows, gla[1, :, :, cols].reshape(1024, 384), preferred_element_type=F32
        )
        value = value.reshape(4, SUB, 384)
        total = gpa[0, :, cols]
        for i in range(1, 8):
            total = total + gpa[i, :, cols]
        xg[j] = jnp.broadcast_to(total, (8, 384))
        if d:
            outgoing(j)[...] = value.astype(outgoing(j).dtype)
            send_down(j, d, 0)
            dg_copies.append(send(xg.at[j], xgr.at[j], dg_s.at[j], dg_r.at[j], device(x + d, y, z, c)))
        else:
            xo[...] = value
    for h in (1, 2):
        for j, d in enumerate((2, 1, 3)):
            send_down(j, d, h)
    sends += list(d_copies.values()) + dg_copies

    np_[1, 1].wait_recv()
    nm[1, 0].wait_recv()
    nf[1, 0].wait_recv()
    nf[1, 1].wait_recv()
    sends += list(np_.values()) + list(nm.values()) + list(nf.values())
    u_copies = {}
    for n in range(6):

        def second(i, _):
            cols = pl.ds(pl.multiple_of(n * 256 + i * 256, 256), 256)
            g[:, cols] = g[:, cols] + product(1 - zh, cols)
            return 0

        lax.fori_loop(0, 1, second, 0)
        cols = pl.ds(n * 256, 256)
        for j, d in enumerate((2, 1, 3)):
            ty = lax.rem(y + d, 4)
            for k in range(4):
                rows = pl.ds(pl.multiple_of((k * 4 + ty) * 48, 16), 48)
                us[n, j, k] = g[rows, cols].astype(BF16)
            u_copies[n, j] = send(us.at[n, j], ur.at[n, j], u_s.at[n, j], u_r.at[n, j], device(x, y + d, z, c))
    sends += list(u_copies.values())

    v_copies = {}

    def narrow(n):
        cols = pl.ds(n * 256, 256)
        for j in range(3):
            u_copies[n, j].wait_recv()
        for k in range(4):
            rows = pl.ds(pl.multiple_of((k * 4 + y) * 48, 16), 48)
            total = g[rows, cols]
            for j in range(3):
                total = total + ur[n, j, k].astype(F32)
            g[rows, cols] = total
            vs[n, k] = total.astype(BF16)
        for d in (2, 1, 3):
            to = lax.rem(zl + d, 4)
            v_copies[n, d] = send(
                vs.at[n, to], vr.at[n, d - 1], v_s.at[n, d - 1], v_r.at[n, d - 1], device(x, y, zh * 4 + to, c)
            )

    e_copies = {}

    def deliver(h, buffer, landing):
        begin, size = PARTS[h]
        for j in range(3):
            d_copies[j, h].wait_recv()
        for b in range(4):
            total = xo[b, begin : begin + size, :]
            for j in range(3):
                total = total + arrived(j)[b, begin : begin + size, :].astype(F32)
            xo[b, begin : begin + size, :] = total
            for a in range(2):
                at, mid = a * 192, begin + size // 2
                i = a * 4 + b
                buffer[i, 0:size, :] = xo[b, begin : begin + size, at : at + 128]
                buffer[i, size : size + size // 2, 0:64] = xo[b, begin:mid, at + 128 : at + 192]
                buffer[i, size : size + size // 2, 64:128] = xo[b, mid : begin + size, at + 128 : at + 192]
        if h == 2:
            for copy in dg_copies:
                copy.wait_recv()
            total = xg[3]
            for j in range(3):
                total = total + xgr[j]
            xg[3] = total
            for a in range(2):
                for b in range(4):
                    buffer[a * 4 + b, 24:32, :] = jnp.zeros((8, 128), F32)
                    buffer[a * 4 + b, 24:25, :] = xg[3, 0:1, a * 192 : a * 192 + 128]
                    buffer[a * 4 + b, 25:26, 0:64] = xg[3, 0:1, a * 192 + 128 : a * 192 + 192]
        for d in (4, 3, 5, 2, 6, 1, 7):
            e_copies[h, d] = send(
                buffer.at[lax.rem(z + d, 8)], landing.at[d - 1],
                e_s.at[h, d - 1], e_r.at[h, d - 1], device(x, y, z + d, c),
            )

    narrow(0)
    deliver(0, ea, ear)
    narrow(1)
    narrow(2)
    deliver(1, eb, ebr)
    narrow(3)
    deliver(2, ec, ecr)
    narrow(4)
    narrow(5)
    sends += list(v_copies.values()) + list(e_copies.values())

    for h, (buffer, landing) in enumerate(((ea, ear), (eb, ebr), (ec, ecr))):
        begin, size = PARTS[h]
        for d in range(1, 8):
            e_copies[h, d].wait_recv()
        total = buffer[z]
        for j in range(7):
            total = total + landing[j]
        half = size // 2
        gd_out[begin : begin + size, 0:128] = total[0:size]
        gd_out[begin : begin + half, 128:192] = total[size : size + half, 0:64]
        gd_out[begin + half : begin + size, 128:192] = total[size : size + half, 64:128]
        if h == 2:
            gg_out[:, 0:128] = total[24:25]
            gg_out[:, 128:192] = total[25:26, 0:64]
    my_rows = pl.ds(pl.multiple_of((zl * 4 + y) * 48, 16), 48)
    for n in range(6):
        cols = pl.ds(n * 256, 256)
        for d in (1, 2, 3):
            v_copies[n, d].wait_recv()
        total = g[my_rows, cols]
        for j in range(3):
            total = total + vr[n, j].astype(F32)
        gu_out[:, cols] = total
    sends += [n_copies[j, 1] for j in range(3)] + [q_copy] + l_copies + wy
    for group in (za, zb, yp, ym, yf, wu, wd):
        sends += list(group.values())
    for copy in sends:
        copy.wait_send()


VMEM = pl.BlockSpec(memory_space=pltpu.VMEM)
ANY = pl.BlockSpec(memory_space=pl.ANY)


def dma(*shape):
    return pltpu.SemaphoreType.DMA(shape) if shape else pltpu.SemaphoreType.DMA


def pairs(*shapes):
    return [dma(*shape) for shape in shapes for _ in range(2)]


def local(hidden, w_down, norm_gain, w_up, grad_query):
    grad_down, grad_up, grad_gain = pl.pallas_call(
        whole,
        out_shape=(
            jax.ShapeDtypeStruct((112, 192), F32),
            jax.ShapeDtypeStruct((48, 1536), F32),
            jax.ShapeDtypeStruct((1, 192), F32),
        ),
        in_specs=[ANY, ANY, VMEM, ANY, ANY],
        out_specs=(VMEM, VMEM, VMEM),
        scratch_shapes=[
            pltpu.VMEM((128, 3584), BF16),
            pltpu.VMEM((192, 256), BF16),
            pltpu.VMEM((1536, 1536), BF16),
            pltpu.VMEM((8, 2, 128, 1536), BF16),
            pltpu.VMEM((256, 192), BF16),
            pltpu.VMEM((2, 128, 1792), BF16),
            pltpu.VMEM((4, SUB, 192), BF16),
            pltpu.VMEM((2, 4, 1, 192), F32),
            pltpu.VMEM((2, 4, 4, SUB, 768), BF16),
            pltpu.VMEM((3, 256, 1536), BF16),
            pltpu.VMEM((3, 256, 1536), BF16),
            pltpu.VMEM((256, 1536), F32),
            pltpu.VMEM((128, 1536), BF16),
            pltpu.VMEM((128, 1536), BF16),
            pltpu.VMEM((2, 2, 128, 768), F32),
            pltpu.VMEM((2, 128, 768), F32),
            pltpu.VMEM((128, 1536), F32),
            pltpu.VMEM((4, 4, 2, SUB, 128), BF16),
            pltpu.VMEM((1536, 128), BF16),
            pltpu.VMEM((16, 48, 128), BF16),
            pltpu.VMEM((8, 16, 48, 256), BF16),
            pltpu.VMEM((2, 8, 128, 1536), BF16),
            pltpu.VMEM((8, 1, 1536), F32),
            pltpu.VMEM((4, SUB, 1024), BF16),
            pltpu.VMEM((768, 1536), F32),
            pltpu.VMEM((4, SUB, 384), BF16),
            pltpu.VMEM((2, 4, SUB, 384), F32),
            pltpu.VMEM((4, SUB, 384), F32),
            pltpu.VMEM((4, SUB, 384), BF16),
            pltpu.VMEM((2, 4, SUB, 384), F32),
            pltpu.VMEM((4, 8, 384), F32),
            pltpu.VMEM((3, 8, 384), F32),
            pltpu.VMEM((8, 72, 128), F32),
            pltpu.VMEM((7, 72, 128), F32),
            pltpu.VMEM((8, 72, 128), F32),
            pltpu.VMEM((7, 72, 128), F32),
            pltpu.VMEM((8, 32, 128), F32),
            pltpu.VMEM((7, 32, 128), F32),
            pltpu.VMEM((6, 3, 4, 48, 256), BF16),
            pltpu.VMEM((6, 3, 4, 48, 256), BF16),
            pltpu.VMEM((6, 4, 48, 256), BF16),
            pltpu.VMEM((6, 3, 48, 256), BF16),
            dma(8),
        ]
        + pairs((3,), (4,), (), (3, 2), (), (4,), (3,), (8,), (8,), (8,), (2,))
        + pairs((2,), (7,), (2,), (2,), (2,), (4, 2), (7,), (2,), (2, 2), (2, 2), (2, 2), (3, 3), (3,), (3, 7))
        + pairs((6, 3), (6, 4), (3,), (4,), (3,)),
        compiler_params=pltpu.CompilerParams(
            collective_id=0, has_side_effects=True, vmem_limit_bytes=62 * 2**20
        ),
    )(hidden, w_down.T, norm_gain.reshape(1, 192), w_up, grad_query.reshape(8, 128, 1536))
    return grad_down, grad_up, grad_gain.reshape(192)


def solution(mesh):
    placed = (P(("dp", "st"), None), P(None, "st"), P("st"), P(None, "st"), P("dp", "st"))
    return jax.shard_map(
        local,
        mesh=mesh,
        in_specs=placed,
        out_specs=(P("dp", "st"), P("dp", "st"), P("st")),
        check_vma=False,
    )
```
